128 devices in a mesh: gx: 8 (over z, core), gy: 4 (over x), gz: 4 (over y).
Axes of the slice: x: 4, y: 4, z: 4, core: 2. Of those that a mesh axis runs over, the one named last changes fastest.
Arguments:
- residual: float32 [4, 256, 64, 512], P(None, 'gx', 'gy', 'gz'), may hold values from -6 to 6
- fdm_vectors: float32 [3, 10, 10, 16384], P(None, None, None, ('gx', 'gy', 'gz')), may hold values from -2 to 2
- fdm_values: float32 [3, 10, 16384], P(None, None, ('gx', 'gy', 'gz')), may hold values from 0.2 to 4
- corner_vertex: int32 [8, 16384], P(None, ('gx', 'gy', 'gz')), may hold values from 0 to 511
- own_factor: float32 [65536, 512], P(('gx', 'gy', 'gz')), may hold values from -0.0625 to 0.0625
- sep_factor: float32 [65536, 128], P(('gx', 'gy', 'gz')), may hold values from -0.109375 to 0.109375
- sep_cols: int32 [65536, 128], P(('gx', 'gy', 'gz')), may hold values from 0 to 21503, as said below
Outputs:
- preconditioned: float32 [4, 256, 64, 512], P(None, 'gx', 'gy', 'gz')
The draws below stay inside these ranges and needn't reach their ends.
Inputs may be any that keep to these rules, and one draw needn't show every extreme that they name: `sep_cols`: in each row the first 32 entries name line separator columns, the next 32 plane separator columns, the rest top separator columns.
All inputs are finite; a program needn't handle non-finite values.
Results may differ from the reference program's by a relative error of at most 0.0003.
Values sent between devices are 32-bit elements; how exact they have to be, the bound alone decides.
No kernel may reach another device: no remote copies, remote signals or barrier semaphores. Data moves between devices by JAX's collectives and lax.ppermute only.
A program may use at most 320 MiB of HBM per device.

```python
import math
import jax
import jax.numpy as jnp
from jax import lax

NODE = 8
EX = 4
EY = 2
EZ = 16
NRHS = 4
VERTS = 512
LINE_SEP = 1024
PLANE_SEP = 4096
TOP_SEP = 16384
ROW_NNZ = 128
SEPS = 21504
ELEMS = 128
ALL_ELEMS = 16384
ROWS = 65536
GRID_X = 256
GRID_Y = 64
GRID_Z = 512
N_GX = 8
N_GY = 4
N_GZ = 4


def draw_sep_cols(key, part):
    key = jax.random.fold_in(key, 7)
    quarter = ROW_NNZ // 4
    first_key, second_key, third_key = jax.random.split(key, 3)
    line = jax.random.randint(first_key, (ROWS, quarter), 0, LINE_SEP)
    plane = LINE_SEP + jax.random.randint(second_key, (ROWS, quarter), 0, PLANE_SEP)
    top = LINE_SEP + PLANE_SEP + jax.random.randint(third_key, (ROWS, ROW_NNZ - 2 * quarter), 0, TOP_SEP)
    return jnp.concatenate([line, plane, top], axis=1).astype(jnp.int32)


def touch_ends(values, rng, smallest, high):
    spot = [jax.random.randint(jax.random.fold_in(rng, axis), (), 0, length) for axis, length in enumerate(values.shape)]
    longest = values.shape.index(max(values.shape))
    beside = spot[:longest] + [(spot[longest] + 1) % values.shape[longest]] + spot[longest + 1:]
    return values.at[tuple(spot)].set(smallest).at[tuple(beside)].set(high)


def steps_of(key, dims, pieces, low, largest):
    loudness, own = 1.0, jax.random.fold_in(key, 6)
    for position, parts in pieces:
        heights = jnp.exp(jax.random.uniform(jax.random.fold_in(own, position), (parts,), jnp.float32, low / len(pieces), largest / len(pieces)))
        loudness = loudness * jnp.repeat(heights, dims[position] // parts).reshape([-1 if axis == position else 1 for axis in range(len(dims))])
    return loudness


def gaussian(stream_key, shape, deviation, most, cuts=(), held_as=jnp.bfloat16):
    loudness = steps_of(stream_key, shape, cuts, -0.22, 0.18) if cuts else 1.0
    result = jax.random.normal(stream_key, shape, jnp.float32) * deviation * loudness
    return jnp.minimum(jnp.maximum(result, -most), most).astype(held_as)


def setup_inputs(seed: int = 0) -> dict:
    arg_keys = jax.random.split(jax.random.key(seed), 8)
    return {
        "residual": gaussian(arg_keys[0], (NRHS, GRID_X, GRID_Y, GRID_Z), 1.0, 6.0, ((1, 8), (2, 4), (3, 4)), jnp.float32),
        "fdm_vectors": gaussian(arg_keys[1], (3, NODE + 2, NODE + 2, ALL_ELEMS), (NODE + 2) ** -0.5, 2.0, ((3, 128),), jnp.float32),
        "fdm_values": jnp.clip(jnp.exp(math.log(4.0) - 2.9957323 * jax.random.uniform(arg_keys[2], (3, NODE + 2, ALL_ELEMS), jnp.float32) ** steps_of(arg_keys[2], (3, NODE + 2, ALL_ELEMS), ((2, 128),), -0.2, 0.2)), 0.2, 4.0),
        "corner_vertex": touch_ends(jax.random.randint(arg_keys[3], (8, ALL_ELEMS), 0, VERTS), jax.random.fold_in(arg_keys[3], 1), 0, VERTS - 1).astype(jnp.int32),
        "own_factor": gaussian(arg_keys[4], (ROWS, VERTS), (16 * VERTS) ** -0.5, 0.0625, ((0, 128),), jnp.float32),
        "sep_factor": gaussian(arg_keys[5], (ROWS, ROW_NNZ), (24 * ROW_NNZ) ** -0.5, 0.109375, ((0, 128),), jnp.float32),
        "sep_cols": draw_sep_cols(jax.random.fold_in(arg_keys[7], 71), 0),
    }


precise = lax.Precision.HIGHEST


def corner_table():
    spacing = jnp.arange(NODE, dtype=jnp.float32) / (NODE - 1)
    return jnp.stack([1.0 - spacing, spacing])


def vertex_loads(field, corner_vertex, weights):
    vectors, size_x, size_y, size_z = field.shape
    cells = field.reshape(vectors, size_x // NODE, NODE, size_y // NODE, NODE, size_z // NODE, NODE)
    load = jnp.einsum('naibjck,pi,qj,rk->npqrabc', cells, weights, weights, weights, precision=precise)
    flat = load.reshape(vectors, -1)
    summed = jax.ops.segment_sum(flat.T, corner_vertex.reshape(-1), num_segments=VERTS)
    return summed.T


def separator_terms(sep_factor, sep_cols, loads):
    vectors = loads.shape[0]
    terms = sep_factor[None, :, :] * loads[:, :, None]
    summed = jax.ops.segment_sum(terms.reshape(vectors, -1).T, sep_cols.reshape(-1), num_segments=SEPS)
    return summed.T


def coarse_values(own_factor, sep_factor, sep_cols, own_coef, sep_coef):
    direct = jnp.einsum('vw,nw->nv', own_factor, own_coef, precision=precise)
    picked = sep_coef[:, sep_cols]
    return direct + jnp.einsum('vk,nvk->nv', sep_factor, picked, precision=precise)


def spread(values, corner_vertex, weights, counts):
    vectors = values.shape[0]
    corners = values[:, corner_vertex.reshape(-1)].reshape((vectors, 2, 2, 2) + counts)
    nodal = jnp.einsum('npqrabc,pi,qj,rk->naibjck', corners, weights, weights, weights, precision=precise)
    return nodal.reshape(vectors, counts[0] * NODE, counts[1] * NODE, counts[2] * NODE)


def widen(field, axis, count):
    size = count * NODE
    core = lax.slice_in_dim(field, 1, size + 1, 1, axis)
    core = core.reshape(field.shape[:axis] + (count, NODE) + field.shape[axis + 1:])
    before = jnp.expand_dims(lax.slice_in_dim(field, 0, size, NODE, axis), axis + 1)
    after = jnp.expand_dims(lax.slice_in_dim(field, NODE + 1, size + 2, NODE, axis), axis + 1)
    return jnp.concatenate([before, core, after], axis=axis + 1)


def diagonal_solve(windows, vectors_fdm, values_fdm):
    first = vectors_fdm[0]
    second = vectors_fdm[1]
    third = vectors_fdm[2]
    work = jnp.einsum('aie,ajkne->ijkne', first, windows, precision=precise)
    work = jnp.einsum('bje,ibkne->ijkne', second, work, precision=precise)
    work = jnp.einsum('cke,ijcne->ijkne', third, work, precision=precise)
    spectrum = values_fdm[0][:, None, None, :] + values_fdm[1][None, :, None, :] + values_fdm[2][None, None, :, :]
    work = work / spectrum[:, :, :, None, :]
    work = jnp.einsum('iae,ajkne->ijkne', first, work, precision=precise)
    work = jnp.einsum('jbe,ibkne->ijkne', second, work, precision=precise)
    work = jnp.einsum('kce,ijcne->ijkne', third, work, precision=precise)
    return work


def schwarz(padded, vectors_fdm, values_fdm, counts):
    vectors = padded.shape[0]
    extent = NODE + 2
    wide = widen(padded, 1, counts[0])
    wide = widen(wide, 3, counts[1])
    wide = widen(wide, 5, counts[2])
    windows = wide.transpose(2, 4, 6, 0, 1, 3, 5).reshape(extent, extent, extent, vectors, -1)
    solved = diagonal_solve(windows, vectors_fdm, values_fdm)
    inner = solved[1:NODE + 1, 1:NODE + 1, 1:NODE + 1].reshape((NODE, NODE, NODE, vectors) + counts)
    return inner.transpose(3, 4, 0, 5, 1, 6, 2).reshape(vectors, counts[0] * NODE, counts[1] * NODE, counts[2] * NODE)


def reference(residual, fdm_vectors, fdm_values, corner_vertex, own_factor, sep_factor, sep_cols):
    weights = corner_table()
    counts = (EX, EY, EZ)
    devices = N_GX * N_GY * N_GZ
    local_x = NODE * EX
    local_y = NODE * EY
    local_z = NODE * EZ
    extent = NODE + 2
    blocks = residual.reshape(NRHS, N_GX, local_x, N_GY, local_y, N_GZ, local_z)
    blocks = blocks.transpose(1, 3, 5, 0, 2, 4, 6).reshape(devices, NRHS, local_x, local_y, local_z)
    corners_all = corner_vertex.reshape(8, devices, ELEMS).transpose(1, 0, 2)
    loads = jax.vmap(lambda block, corners: vertex_loads(block, corners, weights))(blocks, corners_all)
    own_all = own_factor.reshape(devices, VERTS, VERTS)
    sep_all = sep_factor.reshape(devices, VERTS, ROW_NNZ)
    cols_all = sep_cols.reshape(devices, VERTS, ROW_NNZ)
    own_coef = jnp.einsum('dvw,dnv->dnw', own_all, loads, precision=precise)
    partial_value = jax.vmap(separator_terms)(sep_all, cols_all, loads)
    grid = partial_value.reshape(N_GX, N_GY, N_GZ, NRHS, SEPS)
    line = jnp.sum(grid[..., :LINE_SEP], axis=2)
    plane = jnp.sum(grid[..., LINE_SEP:LINE_SEP + PLANE_SEP], axis=(1, 2))
    top = jnp.sum(grid[..., LINE_SEP + PLANE_SEP:], axis=(0, 1, 2))
    line_all = jnp.broadcast_to(line[:, :, None], (N_GX, N_GY, N_GZ, NRHS, LINE_SEP))
    plane_all = jnp.broadcast_to(plane[:, None, None], (N_GX, N_GY, N_GZ, NRHS, PLANE_SEP))
    top_all = jnp.broadcast_to(top, (N_GX, N_GY, N_GZ, NRHS, TOP_SEP))
    sep_coef = jnp.concatenate([line_all, plane_all, top_all], axis=-1).reshape(devices, NRHS, SEPS)
    solution = jax.vmap(coarse_values)(own_all, sep_all, cols_all, own_coef, sep_coef)
    padded = jnp.pad(residual, ((0, 0), (1, 1), (0, 0), (0, 0)), mode="wrap")
    padded = jnp.pad(padded, ((0, 0), (0, 0), (1, 1), (1, 1)))
    vec_blocks = fdm_vectors.reshape(3, extent, extent, devices, ELEMS).transpose(3, 0, 1, 2, 4)
    val_blocks = fdm_values.reshape(3, extent, devices, ELEMS).transpose(2, 0, 1, 3)
    identities = jnp.arange(devices, dtype=jnp.int32)

    def one_device(items):
        device, vec_block, val_block, values, corners = items
        row_x = device // (N_GY * N_GZ)
        row_y = (device // N_GZ) % N_GY
        row_z = device % N_GZ
        start = (jnp.int32(0), row_x * local_x, row_y * local_y, row_z * local_z)
        piece = lax.dynamic_slice(padded, start, (NRHS, local_x + 2, local_y + 2, local_z + 2))
        return schwarz(piece, vec_block, val_block, counts) + spread(values, corners, weights, counts)

    outs = lax.map(one_device, (identities, vec_blocks, val_blocks, solution, corners_all))
    outs = outs.reshape(N_GX, N_GY, N_GZ, NRHS, local_x, local_y, local_z)
    return outs.transpose(3, 0, 4, 1, 5, 2, 6).reshape(NRHS, GRID_X, GRID_Y, GRID_Z)
```

```python
import functools

import jax
import jax.numpy as jnp
from jax import lax
from jax.experimental import pallas as pl
from jax.experimental.pallas import tpu as pltpu
from jax.sharding import PartitionSpec as P

NODE = 8
VERTS = 512
LINE_SEP = 1024
PLANE_SEP = 4096
AXES = ("gx", "gy", "gz")
F32 = jnp.float32
BF16 = jnp.bfloat16
HIGH = lax.Precision.HIGHEST
VMEM_LIMIT = 48 * 1024 * 1024


def iota(shape, dim):
    return lax.broadcasted_iota(jnp.int32, shape, dim)


def split2(x):
    high = x.astype(BF16)
    return high, (x - high.astype(F32)).astype(BF16)


def dot_t(left, right):
    return lax.dot_general(left, right, (((1,), (1,)), ((), ())), preferred_element_type=F32)


def dot_n(left, right):
    return lax.dot_general(left, right, (((1,), (0,)), ((), ())), preferred_element_type=F32)


def z_weights():
    z = iota((128, 256), 0)
    col = iota((128, 256), 1)
    one = (z % NODE).astype(F32) / (NODE - 1)
    value = jnp.where(col // 128 == 1, one, 1.0 - one)
    return jnp.where(z // NODE == col % 16, value, 0.0)


def one_hot_corners(corner_ref, p, q):
    vertex = iota((VERTS, 128), 0)
    first = p * 4 + q * 2
    sides = [jnp.where(vertex == corner_ref[first + r : first + r + 1, :], 1.0, 0.0).astype(BF16) for r in range(2)]
    return jnp.concatenate(sides, axis=1)


def one_hot_rows(index, rows):
    spread_index = jnp.broadcast_to(index.astype(F32), (rows, VERTS)).astype(BF16)
    return iota((rows, VERTS), 0).astype(F32).astype(BF16) == spread_index


def pick(mask, value):
    return jnp.where(mask, value, jnp.zeros_like(value))


def scatter_step(col, fac, rhs, low_bits, high_rows):
    low = jnp.bitwise_and(col, (1 << low_bits) - 1)
    high = lax.shift_right_logical(col, low_bits)
    low_hot = jnp.where(one_hot_rows(low, 1 << low_bits), jnp.ones((), BF16), jnp.zeros((), BF16))
    mask = one_hot_rows(high, high_rows)
    tops, rests = [], []
    for n in range(4):
        value_high, value_low = split2(fac * rhs[n : n + 1, :])
        shape = (high_rows, VERTS)
        tops.append(pick(mask, jnp.broadcast_to(value_high.astype(F32), shape).astype(BF16)))
        rests.append(pick(mask, jnp.broadcast_to(value_low.astype(F32), shape).astype(BF16)))
    return dot_t(jnp.concatenate(tops + rests, axis=0), low_hot)


def loads_kernel(res_ref, corner_ref, fac_ref, col_ref, out_ref, rhs_ref, col_t_ref, fac_t_ref, rows_ref, top_ref, plane_ref, line_ref):
    node = iota((NODE, 128), 0).astype(F32) / (NODE - 1)
    for n in range(4):
        for a in range(4):
            for b in range(2):
                one = zero = None
                for i in range(NODE):
                    tile = res_ref[n, a * 8 + i, b * 8 : b * 8 + 8, :]
                    if i < NODE - 1:
                        term = tile * (1.0 - i / 7.0)
                        zero = term if zero is None else zero + term
                    if i > 0:
                        term = tile * (i / 7.0)
                        one = term if one is None else one + term
                for p, part in enumerate((zero, one)):
                    row = (p * 4 + n) * 8 + a * 2 + b
                    upper = part * node
                    rows_ref[0, row : row + 1, :] = jnp.sum(part - upper, axis=0, keepdims=True)
                    rows_ref[1, row : row + 1, :] = jnp.sum(upper, axis=0, keepdims=True)
    weights = z_weights()
    own_block = iota((64, 256), 0) % 8 == (iota((64, 256), 1) % 128) // 16
    sums = [None, None]
    for q in range(2):
        spread_out = lax.dot_general(rows_ref[q], weights, (((1,), (0,)), ((), ())), precision=HIGH, preferred_element_type=F32)
        load = jnp.sum(jnp.where(own_block, spread_out, 0.0).reshape(8, 8, 256), axis=1)
        load_high, load_low = split2(load)
        left = jnp.concatenate([load_high, load_low], axis=0)
        for p in range(2):
            part = dot_t(left, one_hot_corners(corner_ref, p, q))
            sums[p] = part if sums[p] is None else sums[p] + part
    rhs = sums[0][0:4] + sums[0][8:12] + sums[1][4:8] + sums[1][12:16]
    rhs_ref[...] = rhs
    col_t_ref[...] = col_ref[...].T
    fac_t_ref[...] = fac_ref[...].T

    top_ref[...] = jnp.zeros_like(top_ref)
    plane_ref[...] = jnp.zeros_like(plane_ref)
    line_ref[...] = jnp.zeros_like(line_ref)

    def run(first, count, unroll, base, low_bits, high_rows, total_ref):
        def body(step, carry):
            for u in range(unroll):
                m = first + step * unroll + u
                col = col_t_ref[pl.ds(m, 1), :] - base
                fac = fac_t_ref[pl.ds(m, 1), :]
                total_ref[...] += scatter_step(col, fac, rhs_ref, low_bits, high_rows)
            return carry

        lax.fori_loop(0, count // unroll, body, 0)

    run(64, 64, 2, LINE_SEP + PLANE_SEP, 8, 64, top_ref)
    run(32, 32, 2, LINE_SEP, 8, 16, plane_ref)
    run(0, 32, 2, 0, 7, 8, line_ref)

    out_ref[...] = jnp.zeros_like(out_ref)
    flat = out_ref.reshape(1024, 128)
    for t in range(32):
        for h in range(2):
            lanes = slice(h * 128, h * 128 + 128)
            tile = top_ref[t * 8 : t * 8 + 8, lanes] + top_ref[256 + t * 8 : 264 + t * 8, lanes]
            slot = 2 * (t * 2 + h)
            out_ref[slot, 0:4, :] = tile[0:4]
            out_ref[slot + 1, 0:4, :] = tile[4:8]
    for t in range(8):
        for h in range(2):
            lanes = slice(h * 128, h * 128 + 128)
            tile = plane_ref[t * 8 : t * 8 + 8, lanes] + plane_ref[64 + t * 8 : 72 + t * 8, lanes]
            flat[pl.ds((t * 2 + h) * 64 + 4, 8, stride=8), :] = tile
    for t in range(4):
        tile = line_ref[t * 8 : t * 8 + 8, :] + line_ref[32 + t * 8 : 40 + t * 8, :]
        flat[pl.ds(t * 64 + 5, 8, stride=8), :] = tile


def sums_kernel(in_ref, out_ref):
    row = iota((8, 128), 0)
    planes, lines = [], []
    for i in range(8):
        group = []
        for j in range(4):
            first = (i * 4 + j) * 4
            group.append((in_ref[first] + in_ref[first + 1]) + (in_ref[first + 2] + in_ref[first + 3]))
        lines.append(group)
        planes.append((group[0] + group[1]) + (group[2] + group[3]))
    top = ((planes[0] + planes[1]) + (planes[2] + planes[3])) + ((planes[4] + planes[5]) + (planes[6] + planes[7]))
    for i in range(8):
        for j in range(4):
            value = jnp.where(row < 4, top, jnp.where(row == 4, planes[i], lines[i][j]))
            for k in range(4):
                out_ref[(i * 4 + j) * 4 + k] = value


def gather_step(table, col, fac, low_bits, high_rows, totals):
    low = jnp.bitwise_and(col, (1 << low_bits) - 1)
    high = lax.shift_right_logical(col, low_bits)
    low_hot = jnp.where(one_hot_rows(low, 1 << low_bits), jnp.ones((), BF16), jnp.zeros((), BF16))
    found = dot_n(table, low_hot)
    mask = iota((high_rows, VERTS), 0) == high
    result = []
    for n in range(4):
        picked = found[n * high_rows : (n + 1) * high_rows] + found[(4 + n) * high_rows : (5 + n) * high_rows]
        picked = jnp.where(mask, picked, 0.0)
        picked = jnp.sum(picked.reshape(high_rows // 8, 8, VERTS), axis=0)
        result.append(totals[n] + picked * fac)
    return tuple(result)


def finish_kernel(sep_ref, own_ref, col_t_ref, fac_t_ref, corner_ref, local_ref, out_ref, top_ref, plane_ref, line_ref, split_ref):
    flat = sep_ref.reshape(1024, 128)

    def put(table_ref, rows, lanes, offset, value):
        high, low = split2(value)
        table_ref[rows, lanes] = high.astype(table_ref.dtype)
        table_ref[slice(rows.start + offset, rows.stop + offset), lanes] = low.astype(table_ref.dtype)

    for t in range(32):
        for h in range(2):
            lanes = slice(h * 128, h * 128 + 128)
            slot = 2 * (t * 2 + h)
            tile = jnp.concatenate([sep_ref[slot, 0:4, :], sep_ref[slot + 1, 0:4, :]], axis=0)
            put(top_ref, slice(t * 8, t * 8 + 8), lanes, 256, tile)
    for t in range(8):
        for h in range(2):
            lanes = slice(h * 128, h * 128 + 128)
            tile = flat[pl.ds((t * 2 + h) * 64 + 4, 8, stride=8), :]
            put(plane_ref, slice(t * 8, t * 8 + 8), lanes, 64, tile)
    for t in range(4):
        tile = flat[pl.ds(t * 64 + 5, 8, stride=8), :]
        put(line_ref, slice(t * 8, t * 8 + 8), slice(0, 128), 32, tile)

    def run(first, count, unroll, base, low_bits, high_rows, table_ref, totals):
        table = table_ref[...].astype(BF16)

        def body(step, carry):
            for u in range(unroll):
                m = first + step * unroll + u
                col = col_t_ref[pl.ds(m, 1), :] - base
                fac = fac_t_ref[pl.ds(m, 1), :]
                carry = gather_step(table, col, fac, low_bits, high_rows, carry)
            return carry

        return lax.fori_loop(0, count // unroll, body, totals)

    totals = tuple(jnp.zeros((8, VERTS), F32) for _ in range(4))
    totals = run(0, 32, 2, 0, 7, 8, line_ref, totals)
    totals = run(32, 32, 2, LINE_SEP, 8, 16, plane_ref, totals)
    totals = run(64, 64, 2, LINE_SEP + PLANE_SEP, 8, 64, top_ref, totals)
    for n in range(4):
        value = jnp.sum(totals[n], axis=0, keepdims=True) + own_ref[n : n + 1, :]
        high, low = split2(value)
        split_ref[n : n + 1, :] = high.astype(F32)
        split_ref[n + 4 : n + 5, :] = low.astype(F32)
    left = split_ref[...].astype(BF16)
    left = jnp.concatenate([left, jnp.zeros_like(left)], axis=0)
    weights = z_weights()
    node = iota((NODE, 128), 0).astype(F32) / (NODE - 1)
    own_block = iota((8, 256), 0) == (iota((8, 256), 1) % 128) // 16
    edges = []
    for p in range(2):
        for q in range(2):
            corners = dot_n(left, one_hot_corners(corner_ref, p, q))
            rows = []
            for n in range(4):
                value = corners[n : n + 1, :] + corners[n + 4 : n + 5, :]
                rows.append(jnp.where(own_block, jnp.broadcast_to(value, (8, 256)), 0.0))
            edges.append(
                lax.dot_general(jnp.concatenate(rows, axis=0), weights, (((1,), (1,)), ((), ())), precision=HIGH, preferred_element_type=F32)
            )
    for n in range(4):
        for a in range(4):
            for b in range(2):
                row = n * 8 + a * 2 + b
                ends = []
                for p in range(2):
                    at_zero = edges[p * 2][row : row + 1, :]
                    step = edges[p * 2 + 1][row : row + 1, :] - at_zero
                    ends.append(at_zero + node * step)
                step = ends[1] - ends[0]
                for i in range(NODE):
                    tile = local_ref[n, a * 8 + i, b * 8 : b * 8 + 8, :]
                    out_ref[n, a * 8 + i, b * 8 : b * 8 + 8, :] = tile + (ends[0] + step * (i / 7.0))


def params():
    return pltpu.CompilerParams(vmem_limit_bytes=VMEM_LIMIT)


def coarse_start(residual, corner_vertex, sep_factor, sep_cols):
    shape = jax.ShapeDtypeStruct
    return pl.pallas_call(
        loads_kernel,
        out_shape=(shape((128, 8, 128), F32), shape((4, VERTS), F32), shape((128, VERTS), jnp.int32), shape((128, VERTS), F32)),
        scratch_shapes=[
            pltpu.VMEM((2, 64, 128), F32),
            pltpu.VMEM((512, 256), F32),
            pltpu.VMEM((128, 256), F32),
            pltpu.VMEM((64, 128), F32),
        ],
        compiler_params=params(),
        name="loads",
    )(residual, corner_vertex, sep_factor, sep_cols)


def middle_sums(parts):
    return pl.pallas_call(sums_kernel, out_shape=jax.ShapeDtypeStruct((128, 8, 128), F32), compiler_params=params(), name="sums")(parts)


def coarse_end(parts, own, col_t, fac_t, corner_vertex, local_part):
    return pl.pallas_call(
        finish_kernel,
        out_shape=jax.ShapeDtypeStruct(local_part.shape, F32),
        scratch_shapes=[
            pltpu.VMEM((512, 256), F32),
            pltpu.VMEM((128, 256), F32),
            pltpu.VMEM((64, 128), F32),
            pltpu.VMEM((8, VERTS), F32),
        ],
        compiler_params=params(),
        name="finish",
    )(parts, own, col_t, fac_t, corner_vertex, local_part)


W_ROWS = 40
INNER = 32


def arrange_kernel(res_ref, x_before_ref, x_after_ref, y_before_ref, y_after_ref, win_ref, high_ref, low_ref, edge_ref, left_ref):
    flat = res_ref.reshape(2048, 128)
    for n in range(4):
        edge_ref[0, n, 0:34, :] = y_before_ref[n]
        edge_ref[3, n, 0:34, :] = y_after_ref[n]
        for side, y in ((1, 7), (2, 8)):
            edge_ref[side, n, 0:1, :] = x_before_ref[n, y : y + 1, :]
            edge_ref[side, n, 1:33, :] = flat[pl.ds(n * 512 + y, 32, stride=16), :]
            edge_ref[side, n, 33:34, :] = x_after_ref[n, y : y + 1, :]

    def tile(n, x, b):
        rows = slice(b * 8, b * 8 + 8)
        if x < 0:
            return x_before_ref[n, rows, :]
        if x > 31:
            return x_after_ref[n, rows, :]
        return res_ref[n, x, rows, :]

    def put(row, block, value):
        high, low = split2(value)
        lanes = slice(block * 128, block * 128 + 128)
        left_ref[row : row + 16, lanes] = high
        left_ref[448 + row : 464 + row, lanes] = low

    for n in range(4):
        for a in range(4):
            for b in range(2):
                for i in range(0, 10, 2):
                    x = a * 8 + i - 1
                    put(n * 80 + i * 8, a * 2 + b, jnp.concatenate([tile(n, x, b), tile(n, x + 1, b)], axis=0))
                for side in range(2):
                    put(320 + (n * 2 + side) * 16, a * 2 + b, edge_ref[side * 2 + b, n, a * 8 : a * 8 + 16, :])

    row = iota((1024, 128), 0)
    z = jnp.bitwise_and(row, 127)
    place = jnp.bitwise_and(z, 7) * 128 + lax.shift_right_logical(row, 7) * 16 + lax.shift_right_logical(z, 3)
    lane = iota((1024, 128), 1)
    for pair in range(4):
        moves = [jnp.where(place == lane + (pair * 2 + h) * 128, 1.0, 0.0).astype(BF16) for h in range(2)]
        moved = dot_n(left_ref[...], jnp.concatenate(moves, axis=1))
        moved = moved[0:448] + moved[448:896]
        for h in range(2):
            base = (pair * 2 + h) * 400
            lanes = slice(h * 128, h * 128 + 128)
            for n in range(4):
                for i in range(10):
                    first = n * 80 + i * 8
                    win_ref[pl.ds(base + i * W_ROWS + 4 + n, 8, stride=4), :] = moved[first : first + 8, lanes]
                for side in range(2):
                    first = 320 + (n * 2 + side) * 16
                    start = base + side * 36 + n
                    win_ref[pl.ds(start, 8, stride=W_ROWS), :] = moved[first : first + 8, lanes]
                    win_ref[start + 320 : start + 321, :] = moved[first + 8 : first + 9, lanes]
                    win_ref[start + 360 : start + 361, :] = moved[first + 9 : first + 10, lanes]

    spot = jnp.bitwise_and(iota((8, 128), 1), 15)
    for group in range(4):
        high = jnp.zeros((8, 128), F32)
        low = jnp.zeros((8, 128), F32)
        for t in range(16):
            at = group * 16 + t
            if at < 50:
                top = win_ref[2800 + at * 8 : 2808 + at * 8, :]
                high = jnp.where(spot == t, pltpu.roll(top, (t - 15) % 128, 1), high)
                bottom = win_ref[at * 8 : at * 8 + 8, :]
                low = jnp.where(spot == t, pltpu.roll(bottom, t, 1), low)
        high_ref[group * 8 : group * 8 + 8, :] = high
        low_ref[group * 8 : group * 8 + 8, :] = low


def solve_kernel(win_ref, before_ref, after_ref, vec_ref, val_ref, out_ref, coef_ref, pair_ref, value_ref, ends_ref, one_ref, two_ref, back_ref):
    eight = (8, 128)
    for d in range(3):
        for r in range(10):
            value_ref[d * 10 + r] = jnp.broadcast_to(val_ref[d, r : r + 1, :], eight)
            for c in range(10):
                coef_ref[d * 100 + r * 10 + c] = jnp.broadcast_to(vec_ref[d, r, c : c + 1, :], eight)
    first_half = iota(eight, 0) < 4

    def halves(one, two):
        return jnp.where(first_half, coef_ref[100 + one[0] * 10 + one[1]], coef_ref[100 + two[0] * 10 + two[1]])

    for m in range(5):
        value_ref[30 + m] = jnp.where(first_half, value_ref[10 + 2 * m], value_ref[11 + 2 * m])
        for k in range(5):
            pair_ref[m * 10 + k * 2] = halves((2 * k, 2 * m), (2 * k + 1, 2 * m + 1))
            pair_ref[m * 10 + k * 2 + 1] = halves((2 * k + 1, 2 * m), (2 * k, 2 * m + 1))
            if m < 4:
                pair_ref[50 + m * 10 + k * 2] = halves((2 * m + 1, 2 * k), (2 * m + 2, 2 * k + 1))
                pair_ref[50 + m * 10 + k * 2 + 1] = halves((2 * m + 1, 2 * k + 1), (2 * m + 2, 2 * k))

    spot = jnp.bitwise_and(iota(eight, 1), 15)
    for at in range(50):
        group = slice(at // 16 * 8, at // 16 * 8 + 8)
        t = at % 16
        rows = slice(at * 8, at * 8 + 8)
        inside = pltpu.roll(win_ref[2800 + at * 8 : 2808 + at * 8, :], 1, 1)
        ends_ref[0, rows, :] = jnp.where(spot == 0, pltpu.roll(before_ref[group, :], (-t) % 128, 1), inside)
        inside = pltpu.roll(win_ref[rows, :], 127, 1)
        ends_ref[1, rows, :] = jnp.where(spot == 15, pltpu.roll(after_ref[group, :], 15 - t, 1), inside)

    def contract(load, store, coef, outs, tiles, chunk):
        for begin in range(0, outs, chunk):
            totals = [[None] * tiles for _ in range(chunk)]
            for r in range(10):
                data = [load(r, t) for t in range(tiles)]
                for o in range(chunk):
                    scale = coef(r, begin + o)
                    for t in range(tiles):
                        term = scale * data[t]
                        totals[o][t] = term if r == 0 else totals[o][t] + term
            for o in range(chunk):
                for t in range(tiles):
                    store(begin + o, t, totals[o][t])

    def along_z(i, carry):
        base = pl.multiple_of(i * W_ROWS, 8)

        def load(r, t):
            if r == 0:
                return ends_ref[0, pl.ds(base + t * 8, 8), :]
            if r == 9:
                return ends_ref[1, pl.ds(base + t * 8, 8), :]
            return win_ref[pl.ds(base + (r - 1) * 400 + t * 8, 8), :]

        def store(o, t, value):
            one_ref[pl.ds(base + o * 400 + t * 8, 8), :] = value

        contract(load, store, lambda r, o: coef_ref[200 + r * 10 + o], 10, 5, 5)
        return carry

    lax.fori_loop(0, 10, along_z, 0)

    def along_x(k, carry):
        base = pl.multiple_of(k * 400, 8)

        def load(r, t):
            return one_ref[pl.ds(base + r * W_ROWS + t * 8, 8), :]

        def store(o, t, value):
            two_ref[pl.ds(base + o * W_ROWS + t * 8, 8), :] = value

        contract(load, store, lambda r, o: coef_ref[r * 10 + o], 10, 5, 5)
        return carry

    lax.fori_loop(0, 10, along_x, 0)

    def along_y(step, carry):
        k = step // 5
        i = (step - k * 5) * 2
        sources = [pl.multiple_of((k * 10 + i + g) * W_ROWS, 8) for g in range(2)]
        data = []
        for g in range(2):
            plain = [two_ref[pl.ds(sources[g] + t * 8, 8), :] for t in range(5)]
            data.append([(v, pltpu.roll(v, 4, 0)) for v in plain])
        sums = [value_ref[20 + k] + value_ref[i + g] for g in range(2)]
        solved = [[], []]
        for m in range(5):
            totals = [None, None]
            for r in range(5):
                for c in range(2):
                    scale = pair_ref[m * 10 + r * 2 + c]
                    for g in range(2):
                        term = scale * data[g][r][c]
                        totals[g] = term if totals[g] is None else totals[g] + term
            for g in range(2):
                value = totals[g] / (sums[g] + value_ref[30 + m])
                solved[g].append((value, pltpu.roll(value, 4, 0)))
        for m in range(4):
            totals = [None, None]
            for r in range(5):
                for c in range(2):
                    scale = pair_ref[50 + m * 10 + r * 2 + c]
                    for g in range(2):
                        term = scale * solved[g][r][c]
                        totals[g] = term if totals[g] is None else totals[g] + term
            for g in range(2):
                target = pl.multiple_of((k * 10 + i + g) * INNER, 8)
                one_ref[pl.ds(target + m * 8, 8), :] = totals[g]
        return carry

    lax.fori_loop(0, 50, along_y, 0)

    def back_x(k, carry):
        base = pl.multiple_of(k * 320, 8)
        target = pl.multiple_of(k * 256, 8)

        def load(r, t):
            return one_ref[pl.ds(base + r * INNER + t * 8, 8), :]

        def store(o, t, value):
            two_ref[pl.ds(target + o * INNER + t * 8, 8), :] = value

        contract(load, store, lambda r, o: coef_ref[(o + 1) * 10 + r], 8, 4, 4)
        return carry

    lax.fori_loop(0, 10, back_x, 0)

    def back_z(i, carry):
        base = pl.multiple_of(i * INNER, 8)

        def load(r, t):
            return two_ref[pl.ds(base + r * 256 + t * 8, 8), :]

        def store(o, t, value):
            one_ref[pl.ds(base + o * 256 + t * 8, 8), :] = value

        contract(load, store, lambda r, o: coef_ref[200 + (o + 1) * 10 + r], 8, 4, 4)
        return carry

    lax.fori_loop(0, 8, back_z, 0)

    for k in range(8):
        lanes = slice(k * 128, k * 128 + 128)
        for n in range(4):
            for i in range(0, 8, 2):
                pieces = [one_ref[pl.ds(k * 256 + (i + g) * INNER + n, 8, stride=4), :] for g in range(2)]
                high, low = split2(jnp.concatenate(pieces, axis=0))
                row = n * 64 + i * 8
                back_ref[row : row + 16, lanes] = high
                back_ref[256 + row : 272 + row, lanes] = low

    row = iota((1024, 128), 0)
    element = jnp.bitwise_and(row, 127)
    place = lax.shift_right_logical(element, 4) * 128 + jnp.bitwise_and(element, 15) * 8 + lax.shift_right_logical(row, 7)
    lane = iota((1024, 128), 1)
    for a in range(4):
        moves = [jnp.where(place == lane + (a * 2 + b) * 128, 1.0, 0.0).astype(BF16) for b in range(2)]
        moved = dot_n(back_ref[...], jnp.concatenate(moves, axis=1))
        moved = moved[0:256] + moved[256:512]
        for b in range(2):
            for n in range(4):
                for i in range(8):
                    first = n * 64 + i * 8
                    out_ref[n, a * 8 + i, b * 8 : b * 8 + 8, :] = moved[first : first + 8, b * 128 : b * 128 + 128]


def pairs(axis, wrap):
    size = lax.axis_size(axis)
    up = [(i, (i + 1) % size) for i in range(size if wrap else size - 1)]
    return up, [(j, i) for i, j in up]


def exchange(last, leading, axis, wrap):
    up, down = pairs(axis, wrap)
    return lax.ppermute(last, axis, up), lax.ppermute(leading, axis, down)


def arrange(residual, x_before, x_after, y_before, y_after):
    shape = jax.ShapeDtypeStruct
    return pl.pallas_call(
        arrange_kernel,
        out_shape=(shape((3200, 128), F32), shape((32, 128), F32), shape((32, 128), F32)),
        scratch_shapes=[pltpu.VMEM((4, 4, 40, 128), F32), pltpu.VMEM((896, 1024), BF16)],
        compiler_params=params(),
        name="arrange",
    )(residual, x_before, x_after, y_before, y_after)


def solve(windows, z_before, z_after, fdm_vectors, fdm_values, shape):
    return pl.pallas_call(
        solve_kernel,
        out_shape=jax.ShapeDtypeStruct(shape, F32),
        scratch_shapes=[
            pltpu.VMEM((300, 8, 128), F32),
            pltpu.VMEM((90, 8, 128), F32),
            pltpu.VMEM((35, 8, 128), F32),
            pltpu.VMEM((2, 400, 128), F32),
            pltpu.VMEM((4000, 128), F32),
            pltpu.VMEM((4000, 128), F32),
            pltpu.VMEM((512, 1024), BF16),
        ],
        compiler_params=params(),
        name="solve",
    )(windows, z_before, z_after, fdm_vectors, fdm_values)


def body(residual, fdm_vectors, fdm_values, corner_vertex, own_factor, sep_factor, sep_cols):
    x_before, x_after = exchange(residual[:, -1], residual[:, 0], "gx", True)
    parts, rhs, col_t, fac_t = coarse_start(residual, corner_vertex, sep_factor, sep_cols)
    parts = lax.all_to_all(parts, AXES, 0, 0)
    y_last = jnp.concatenate([x_before[:, None, -1], residual[:, :, -1], x_after[:, None, -1]], axis=1)
    y_leading = jnp.concatenate([x_before[:, None, 0], residual[:, :, 0], x_after[:, None, 0]], axis=1)
    y_before, y_after = exchange(y_last, y_leading, "gy", False)
    windows, z_last, z_leading = arrange(residual, x_before, x_after, y_before, y_after)
    z_before, z_after = exchange(z_last, z_leading, "gz", False)
    parts = middle_sums(parts)
    parts = lax.all_to_all(parts, AXES, 0, 0)
    own_coef = jnp.einsum("vw,nv->nw", own_factor, rhs, precision=HIGH)
    own = jnp.einsum("vw,nw->nv", own_factor, own_coef, precision=HIGH)
    local_part = solve(windows, z_before, z_after, fdm_vectors, fdm_values, residual.shape)
    return coarse_end(parts, own, col_t, fac_t, corner_vertex, local_part)


def solution(mesh):
    return jax.shard_map(
        body,
        mesh=mesh,
        in_specs=(
            P(None, AXES[0], AXES[1], AXES[2]),
            P(None, None, None, AXES),
            P(None, None, AXES),
            P(None, AXES),
            P(AXES, None),
            P(AXES, None),
            P(AXES, None),
        ),
        out_specs=P(None, AXES[0], AXES[1], AXES[2]),
        check_vma=False,
    )
```

```python
import functools

import jax
import jax.numpy as jnp
from jax import lax
from jax.experimental import pallas as pl
from jax.experimental.pallas import tpu as pltpu
from jax.sharding import PartitionSpec as P

NODE = 8
VERTS = 512
LINE_SEP = 1024
PLANE_SEP = 4096
AXES = ("gx", "gy", "gz")
F32 = jnp.float32
BF16 = jnp.bfloat16
HIGH = lax.Precision.HIGHEST
MIB = 1024 * 1024


def iota(shape, dim):
    return lax.broadcasted_iota(jnp.int32, shape, dim)


def split2(x):
    high = x.astype(BF16)
    return high, (x - high.astype(F32)).astype(BF16)


def dot_t(left, right):
    return lax.dot_general(left, right, (((1,), (1,)), ((), ())), preferred_element_type=F32)


def dot_n(left, right):
    return lax.dot_general(left, right, (((1,), (0,)), ((), ())), preferred_element_type=F32)


def z_weights():
    z = iota((128, 256), 0)
    col = iota((128, 256), 1)
    one = (z % NODE).astype(F32) / (NODE - 1)
    value = jnp.where(col // 128 == 1, one, 1.0 - one)
    return jnp.where(z // NODE == col % 16, value, 0.0)


def one_hot_corners(corner_ref, p, q):
    vertex = iota((VERTS, 128), 0)
    first = p * 4 + q * 2
    sides = [jnp.where(vertex == corner_ref[first + r : first + r + 1, :], 1.0, 0.0).astype(BF16) for r in range(2)]
    return jnp.concatenate(sides, axis=1)


def tile_rows(row):
    return jnp.broadcast_to(row, (16, VERTS)).astype(BF16)


def row_masks(index, rows):
    offset = tile_rows(index.astype(F32)) - iota((16, VERTS), 0).astype(F32).astype(BF16)
    return [offset == jnp.full((16, VERTS), 16.0 * r, BF16) for r in range(rows // 16)]


def one_hot(index, rows):
    one = jnp.ones((16, VERTS), BF16)
    return jnp.concatenate([pick(mask, one) for mask in row_masks(index, rows)], axis=0)


def pick(mask, value):
    return jnp.where(mask, value, jnp.zeros_like(value))


def scatter_step(col, fac, rhs, low_bits, high_rows):
    low_hot = one_hot(jnp.bitwise_and(col, (1 << low_bits) - 1), 1 << low_bits)
    masks = row_masks(lax.shift_right_logical(col, low_bits), high_rows)
    tops, rests = [], []
    for n in range(4):
        value = fac * rhs[n : n + 1, :]
        high = value.astype(BF16).astype(F32)
        high_tile, low_tile = tile_rows(high), tile_rows(value - high)
        tops += [pick(mask, high_tile) for mask in masks]
        rests += [pick(mask, low_tile) for mask in masks]
    return jnp.concatenate(tops + rests, axis=0), low_hot


def loads_kernel(
    res_hbm, corner_ref, fac_hbm, col_hbm, out_ref, rhs_ref, rows_ref, top_ref, plane_ref, line_ref, res_ref, fac_ref, col_ref, col_t_ref, fac_t_ref, sems
):
    fields = [pltpu.make_async_copy(res_hbm.at[n], res_ref.at[n], sems.at[n]) for n in range(4)]
    col_copy = pltpu.make_async_copy(col_hbm, col_ref, sems.at[4])
    fac_copy = pltpu.make_async_copy(fac_hbm, fac_ref, sems.at[5])
    for copy in fields + [col_copy, fac_copy]:
        copy.start()
    node = iota((NODE, 128), 0).astype(F32) / (NODE - 1)
    for n in range(4):
        fields[n].wait()
        for a in range(4):
            for b in range(2):
                one = zero = None
                for i in range(NODE):
                    tile = res_ref[n, a * 8 + i, b * 8 : b * 8 + 8, :]
                    if i < NODE - 1:
                        term = tile * (1.0 - i / 7.0)
                        zero = term if zero is None else zero + term
                    if i > 0:
                        term = tile * (i / 7.0)
                        one = term if one is None else one + term
                for p, part in enumerate((zero, one)):
                    row = (p * 4 + n) * 8 + a * 2 + b
                    upper = part * node
                    rows_ref[0, row : row + 1, :] = jnp.sum(part - upper, axis=0, keepdims=True)
                    rows_ref[1, row : row + 1, :] = jnp.sum(upper, axis=0, keepdims=True)
    weights = z_weights()
    own_block = iota((64, 256), 0) % 8 == (iota((64, 256), 1) % 128) // 16
    sums = [None, None]
    for q in range(2):
        spread_out = lax.dot_general(rows_ref[q], weights, (((1,), (0,)), ((), ())), precision=HIGH, preferred_element_type=F32)
        load = jnp.sum(jnp.where(own_block, spread_out, 0.0).reshape(8, 8, 256), axis=1)
        load_high, load_low = split2(load)
        left = jnp.concatenate([load_high, load_low], axis=0)
        for p in range(2):
            part = dot_t(left, one_hot_corners(corner_ref, p, q))
            sums[p] = part if sums[p] is None else sums[p] + part
    rhs = sums[0][0:4] + sums[0][8:12] + sums[1][4:8] + sums[1][12:16]
    rhs_ref[...] = rhs
    col_copy.wait()
    col_t_ref[...] = col_ref[...].T
    fac_copy.wait()
    fac_t_ref[...] = fac_ref[...].T

    top_ref[...] = jnp.zeros_like(top_ref)
    plane_ref[...] = jnp.zeros_like(plane_ref)
    line_ref[...] = jnp.zeros_like(line_ref)

    def run(first, count, unroll, base, low_bits, high_rows, total_ref):
        def body(step, carry):
            lefts, rights = [], []
            for u in range(unroll):
                m = first + step * unroll + u
                col = col_t_ref[pl.ds(m, 1), :] - base
                fac = fac_t_ref[pl.ds(m, 1), :]
                left, right = scatter_step(col, fac, rhs_ref, low_bits, high_rows)
                lefts.append(left)
                rights.append(right)
            total_ref[...] += dot_t(jnp.concatenate(lefts, axis=1), jnp.concatenate(rights, axis=1))
            return carry

        lax.fori_loop(0, count // unroll, body, 0)

    run(64, 64, 16, LINE_SEP + PLANE_SEP, 8, 64, top_ref)
    run(32, 32, 16, LINE_SEP, 8, 16, plane_ref)
    run(0, 32, 16, 0, 6, 16, line_ref)

    out_ref[...] = jnp.zeros_like(out_ref)
    flat = out_ref.reshape(1024, 128)
    for t in range(32):
        for h in range(2):
            lanes = slice(h * 128, h * 128 + 128)
            tile = top_ref[t * 8 : t * 8 + 8, lanes] + top_ref[256 + t * 8 : 264 + t * 8, lanes]
            slot = 2 * (t * 2 + h)
            out_ref[slot, 0:4, :] = tile[0:4]
            out_ref[slot + 1, 0:4, :] = tile[4:8]
    for t in range(8):
        for h in range(2):
            lanes = slice(h * 128, h * 128 + 128)
            tile = plane_ref[t * 8 : t * 8 + 8, lanes] + plane_ref[64 + t * 8 : 72 + t * 8, lanes]
            flat[pl.ds((t * 2 + h) * 64 + 4, 8, stride=8), :] = tile
    for t in range(8):
        tile = line_ref[t * 8 : t * 8 + 8, :] + line_ref[64 + t * 8 : 72 + t * 8, :]
        flat[pl.ds(t * 64 + 5, 8, stride=8), 0:64] = tile


def sums_kernel(in_ref, order_ref, out_ref):
    row = iota((8, 128), 0)
    planes, lines = [], []
    for i in range(8):
        group = []
        for j in range(4):
            first = (i * 4 + j) * 4
            group.append((in_ref[first] + in_ref[first + 1]) + (in_ref[first + 2] + in_ref[first + 3]))
        lines.append(group)
        planes.append((group[0] + group[1]) + (group[2] + group[3]))
    top = ((planes[0] + planes[1]) + (planes[2] + planes[3])) + ((planes[4] + planes[5]) + (planes[6] + planes[7]))
    for i in range(8):
        for j in range(4):
            value = jnp.where(row < 4, top, jnp.where(row == 4, planes[i], lines[i][j]))
            for k in range(4):
                out_ref[(i * 4 + j) * 4 + k] = value


def gather_step(table, col, fac, low_bits, high_rows, totals):
    found = dot_n(table, one_hot(jnp.bitwise_and(col, (1 << low_bits) - 1), 1 << low_bits))
    high = lax.shift_right_logical(col, low_bits)
    offset = jnp.broadcast_to(high, (8, VERTS)) - iota((8, VERTS), 0)
    result = []
    for n in range(4):
        total = None
        for r in range(high_rows // 8):
            first = n * high_rows + r * 8
            value = found[first : first + 8] + found[4 * high_rows + first : 4 * high_rows + first + 8]
            total = jnp.where(offset == 8 * r, value, 0.0 if total is None else total)
        result.append(totals[n] + total * fac)
    return tuple(result)


def finish_kernel(
    sep_ref, own_ref, col_ref, fac_ref, corner_ref, local_ref, out_ref, top_ref, plane_ref, line_ref, split_ref, col_t_ref, fac_t_ref
):
    col_t_ref[...] = col_ref[...].T
    fac_t_ref[...] = fac_ref[...].T
    flat = sep_ref.reshape(1024, 128)

    def put(table_ref, rows, lanes, offset, value):
        high, low = split2(value)
        table_ref[rows, lanes] = high.astype(table_ref.dtype)
        table_ref[slice(rows.start + offset, rows.stop + offset), lanes] = low.astype(table_ref.dtype)

    for t in range(32):
        for h in range(2):
            lanes = slice(h * 128, h * 128 + 128)
            slot = 2 * (t * 2 + h)
            tile = jnp.concatenate([sep_ref[slot, 0:4, :], sep_ref[slot + 1, 0:4, :]], axis=0)
            put(top_ref, slice(t * 8, t * 8 + 8), lanes, 256, tile)
    for t in range(8):
        for h in range(2):
            lanes = slice(h * 128, h * 128 + 128)
            tile = flat[pl.ds((t * 2 + h) * 64 + 4, 8, stride=8), :]
            put(plane_ref, slice(t * 8, t * 8 + 8), lanes, 64, tile)
    for t in range(8):
        tile = flat[pl.ds(t * 64 + 5, 8, stride=8), 0:64]
        put(line_ref, slice(t * 8, t * 8 + 8), slice(0, 64), 64, tile)

    def run(first, count, unroll, base, low_bits, high_rows, table_ref, totals):
        table = table_ref[...].astype(BF16)

        def body(step, carry):
            for u in range(unroll):
                m = first + step * unroll + u
                col = col_t_ref[pl.ds(m, 1), :] - base
                fac = fac_t_ref[pl.ds(m, 1), :]
                carry = gather_step(table, col, fac, low_bits, high_rows, carry)
            return carry

        return lax.fori_loop(0, count // unroll, body, totals)

    totals = tuple(jnp.zeros((8, VERTS), F32) for _ in range(4))
    totals = run(0, 32, 8, 0, 6, 16, line_ref, totals)
    totals = run(32, 32, 8, LINE_SEP, 8, 16, plane_ref, totals)
    totals = run(64, 64, 16, LINE_SEP + PLANE_SEP, 8, 64, top_ref, totals)
    for n in range(4):
        value = jnp.sum(totals[n], axis=0, keepdims=True) + own_ref[n : n + 1, :]
        high, low = split2(value)
        split_ref[n : n + 1, :] = high.astype(F32)
        split_ref[n + 4 : n + 5, :] = low.astype(F32)
    left = split_ref[...].astype(BF16)
    left = jnp.concatenate([left, jnp.zeros_like(left)], axis=0)
    weights = z_weights()
    node = iota((NODE, 128), 0).astype(F32) / (NODE - 1)
    own_block = iota((8, 256), 0) == (iota((8, 256), 1) % 128) // 16
    edges = []
    for p in range(2):
        for q in range(2):
            corners = dot_n(left, one_hot_corners(corner_ref, p, q))
            rows = []
            for n in range(4):
                value = corners[n : n + 1, :] + corners[n + 4 : n + 5, :]
                rows.append(jnp.where(own_block, jnp.broadcast_to(value, (8, 256)), 0.0))
            edges.append(
                lax.dot_general(jnp.concatenate(rows, axis=0), weights, (((1,), (1,)), ((), ())), precision=HIGH, preferred_element_type=F32)
            )
    for n in range(4):
        for a in range(4):
            for b in range(2):
                row = n * 8 + a * 2 + b
                ends = []
                for p in range(2):
                    at_zero = edges[p * 2][row : row + 1, :]
                    step = edges[p * 2 + 1][row : row + 1, :] - at_zero
                    ends.append(at_zero + node * step)
                step = ends[1] - ends[0]
                for i in range(NODE):
                    tile = local_ref[n, a * 8 + i, b * 8 : b * 8 + 8, :]
                    out_ref[n, a * 8 + i, b * 8 : b * 8 + 8, :] = tile + (ends[0] + step * (i / 7.0))


def params(mib):
    return pltpu.CompilerParams(vmem_limit_bytes=mib * MIB)


def coarse_start(residual, corner_vertex, sep_factor, sep_cols):
    shape = jax.ShapeDtypeStruct
    return pl.pallas_call(
        loads_kernel,
        out_shape=(shape((128, 8, 128), F32), shape((4, VERTS), F32)),
        in_specs=[
            pl.BlockSpec(memory_space=pl.ANY),
            pl.BlockSpec(memory_space=pltpu.VMEM),
            pl.BlockSpec(memory_space=pl.ANY),
            pl.BlockSpec(memory_space=pl.ANY),
        ],
        scratch_shapes=[
            pltpu.VMEM((2, 64, 128), F32),
            pltpu.VMEM((512, 256), F32),
            pltpu.VMEM((128, 256), F32),
            pltpu.VMEM((128, 64), F32),
            pltpu.VMEM((4, 32, 16, 128), F32),
            pltpu.VMEM((512, 128), F32),
            pltpu.VMEM((512, 128), jnp.int32),
            pltpu.VMEM((128, VERTS), jnp.int32),
            pltpu.VMEM((128, VERTS), F32),
            pltpu.SemaphoreType.DMA((6,)),
        ],
        compiler_params=params(60),
        name="loads",
    )(residual, corner_vertex, sep_factor, sep_cols)


def middle_sums(parts, after):
    return pl.pallas_call(
        sums_kernel,
        out_shape=jax.ShapeDtypeStruct((128, 8, 128), F32),
        in_specs=[pl.BlockSpec(memory_space=pltpu.VMEM), pl.BlockSpec(memory_space=pl.ANY)],
        compiler_params=params(16),
        name="sums",
    )(parts, after)


def coarse_end(parts, own, sep_cols, sep_factor, corner_vertex, local_part):
    return pl.pallas_call(
        finish_kernel,
        out_shape=jax.ShapeDtypeStruct(local_part.shape, F32),
        scratch_shapes=[
            pltpu.VMEM((512, 256), F32),
            pltpu.VMEM((128, 256), F32),
            pltpu.VMEM((128, 64), F32),
            pltpu.VMEM((8, VERTS), F32),
            pltpu.VMEM((128, VERTS), jnp.int32),
            pltpu.VMEM((128, VERTS), F32),
        ],
        compiler_params=params(32),
        name="finish",
    )(parts, own, sep_cols, sep_factor, corner_vertex, local_part)


W_ROWS = 40
INNER = 32


def inner_sides(axis):
    index = lax.axis_index(axis)
    return jnp.stack([index > 0, index < lax.axis_size(axis) - 1]).astype(F32)


def masked(flag, value):
    return jnp.where(flag > 0.5, value, 0.0)


def arrange_kernel(flag_ref, res_ref, x_before_ref, x_after_ref, y_before_ref, y_after_ref, order_ref, win_ref, high_ref, low_ref, edge_ref, left_ref):
    flat = res_ref.reshape(2048, 128)
    for n in range(4):
        edge_ref[0, n, 0:34, :] = masked(flag_ref[0], y_before_ref[n])
        edge_ref[3, n, 0:34, :] = masked(flag_ref[1], y_after_ref[n])
        for side, y in ((1, 7), (2, 8)):
            edge_ref[side, n, 0:1, :] = x_before_ref[n, y : y + 1, :]
            edge_ref[side, n, 1:33, :] = flat[pl.ds(n * 512 + y, 32, stride=16), :]
            edge_ref[side, n, 33:34, :] = x_after_ref[n, y : y + 1, :]

    def tile(n, x, b):
        rows = slice(b * 8, b * 8 + 8)
        if x < 0:
            return x_before_ref[n, rows, :]
        if x > 31:
            return x_after_ref[n, rows, :]
        return res_ref[n, x, rows, :]

    def put(row, block, value):
        high, low = split2(value)
        lanes = slice(block * 128, block * 128 + 128)
        left_ref[row : row + 16, lanes] = high
        left_ref[448 + row : 464 + row, lanes] = low

    for n in range(4):
        for a in range(4):
            for b in range(2):
                for i in range(0, 10, 2):
                    x = a * 8 + i - 1
                    put(n * 80 + i * 8, a * 2 + b, jnp.concatenate([tile(n, x, b), tile(n, x + 1, b)], axis=0))
                for side in range(2):
                    put(320 + (n * 2 + side) * 16, a * 2 + b, edge_ref[side * 2 + b, n, a * 8 : a * 8 + 16, :])

    row = iota((1024, 128), 0)
    z = jnp.bitwise_and(row, 127)
    place = jnp.bitwise_and(z, 7) * 128 + lax.shift_right_logical(row, 7) * 16 + lax.shift_right_logical(z, 3)
    lane = iota((1024, 128), 1)
    for pair in range(4):
        moves = [jnp.where(place == lane + (pair * 2 + h) * 128, 1.0, 0.0).astype(BF16) for h in range(2)]
        moved = dot_n(left_ref[...], jnp.concatenate(moves, axis=1))
        moved = moved[0:448] + moved[448:896]
        for h in range(2):
            base = (pair * 2 + h) * 400
            lanes = slice(h * 128, h * 128 + 128)
            for n in range(4):
                for i in range(10):
                    first = n * 80 + i * 8
                    win_ref[pl.ds(base + i * W_ROWS + 4 + n, 8, stride=4), :] = moved[first : first + 8, lanes]
                for side in range(2):
                    first = 320 + (n * 2 + side) * 16
                    start = base + side * 36 + n
                    win_ref[pl.ds(start, 8, stride=W_ROWS), :] = moved[first : first + 8, lanes]
                    win_ref[start + 320 : start + 321, :] = moved[first + 8 : first + 9, lanes]
                    win_ref[start + 360 : start + 361, :] = moved[first + 9 : first + 10, lanes]

    spot = jnp.bitwise_and(iota((8, 128), 1), 15)
    for group in range(4):
        high = jnp.zeros((8, 128), F32)
        low = jnp.zeros((8, 128), F32)
        for t in range(16):
            at = group * 16 + t
            if at < 50:
                top = win_ref[2800 + at * 8 : 2808 + at * 8, :]
                high = jnp.where(spot == t, pltpu.roll(top, (t - 15) % 128, 1), high)
                bottom = win_ref[at * 8 : at * 8 + 8, :]
                low = jnp.where(spot == t, pltpu.roll(bottom, t, 1), low)
        high_ref[group * 8 : group * 8 + 8, :] = high
        low_ref[group * 8 : group * 8 + 8, :] = low


EIGHT = (8, 128)


def fill_coefficients(vec_ref, coef_ref, dims):
    for d in dims:
        for r in range(10):
            for c in range(10):
                coef_ref[d * 100 + r * 10 + c] = jnp.broadcast_to(vec_ref[r, c, d : d + 1, :], EIGHT)


def contract(load, store, coef, outs, tiles, chunk):
    for begin in range(0, outs, chunk):
        totals = [[None] * tiles for _ in range(chunk)]
        for r in range(10):
            data = [load(r, t) for t in range(tiles)]
            for o in range(chunk):
                scale = coef(r, begin + o)
                for t in range(tiles):
                    term = scale * data[t]
                    totals[o][t] = term if r == 0 else totals[o][t] + term
        for o in range(chunk):
            for t in range(tiles):
                store(begin + o, t, totals[o][t])


def fill_pairs(coef_ref, pair_ref, back):
    first_half = iota(EIGHT, 0) < 4

    def halves(one, two):
        return jnp.where(first_half, coef_ref[100 + one[0] * 10 + one[1]], coef_ref[100 + two[0] * 10 + two[1]])

    for m in range(4 if back else 5):
        for k in range(5):
            if back:
                pair_ref[m * 10 + k * 2] = halves((2 * m + 1, 2 * k), (2 * m + 2, 2 * k + 1))
                pair_ref[m * 10 + k * 2 + 1] = halves((2 * m + 1, 2 * k + 1), (2 * m + 2, 2 * k))
            else:
                pair_ref[m * 10 + k * 2] = halves((2 * k, 2 * m), (2 * k + 1, 2 * m + 1))
                pair_ref[m * 10 + k * 2 + 1] = halves((2 * k + 1, 2 * m), (2 * k, 2 * m + 1))


def along_y(source_ref, target_ref, pair_ref, steps, tiles):
    def body(step, carry):
        data = []
        for g in range(2):
            base = pl.multiple_of((step * 2 + g) * W_ROWS, 8)
            plain = [source_ref[pl.ds(base + t * 8, 8), :] for t in range(5)]
            data.append([(v, pltpu.roll(v, 4, 0)) for v in plain])
        for m in range(tiles):
            totals = [None, None]
            for r in range(5):
                for c in range(2):
                    scale = pair_ref[m * 10 + r * 2 + c]
                    for g in range(2):
                        term = scale * data[g][r][c]
                        totals[g] = term if totals[g] is None else totals[g] + term
            for g in range(2):
                target = pl.multiple_of((step * 2 + g) * tiles * 8, 8)
                target_ref[pl.ds(target + m * 8, 8), :] = totals[g]
        return carry

    lax.fori_loop(0, steps, body, 0)


def along_x(source_ref, target_ref, coef_ref, planes):
    def body(k, carry):
        base = pl.multiple_of(k * 400, 8)

        def load(r, t):
            return source_ref[pl.ds(base + r * W_ROWS + t * 8, 8), :]

        def store(o, t, value):
            target_ref[pl.ds(base + o * W_ROWS + t * 8, 8), :] = value

        contract(load, store, lambda r, o: coef_ref[r * 10 + o], 10, 5, 5)
        return carry

    lax.fori_loop(0, planes, body, 0)


def forward_kernel(win_ref, vec_ref, out_ref, coef_ref, pair_ref, work_ref):
    fill_coefficients(vec_ref, coef_ref, (0, 1))
    fill_pairs(coef_ref, pair_ref, False)
    along_x(win_ref, work_ref, coef_ref, 8)
    along_y(work_ref, out_ref, pair_ref, 40, 5)


def solve_kernel(flag_ref, win_ref, inner_ref, before_ref, after_ref, vec_ref, val_ref, out_ref, coef_ref, pair_ref, value_ref, ends_ref, work_ref, one_ref, two_ref, back_ref):
    fill_coefficients(vec_ref, coef_ref, (0, 1, 2))
    fill_pairs(coef_ref, pair_ref, False)
    first_half = iota(EIGHT, 0) < 4
    for d in range(3):
        for r in range(10):
            value_ref[d * 10 + r] = jnp.broadcast_to(val_ref[r, d : d + 1, :], EIGHT)
    for m in range(5):
        value_ref[30 + m] = jnp.where(first_half, value_ref[10 + 2 * m], value_ref[11 + 2 * m])

    spot = jnp.bitwise_and(iota(EIGHT, 1), 15)
    for at in range(50):
        group = slice(at // 16 * 8, at // 16 * 8 + 8)
        t = at % 16
        rows = slice(at * 8, at * 8 + 8)
        inside = pltpu.roll(win_ref[2800 + at * 8 : 2808 + at * 8, :], 1, 1)
        outside = masked(flag_ref[0], pltpu.roll(before_ref[group, :], (-t) % 128, 1))
        ends_ref[rows, :] = jnp.where(spot == 0, outside, inside)
        inside = pltpu.roll(win_ref[rows, :], 127, 1)
        outside = masked(flag_ref[1], pltpu.roll(after_ref[group, :], 15 - t, 1))
        ends_ref[400 + at * 8 : 408 + at * 8, :] = jnp.where(spot == 15, outside, inside)
    along_x(ends_ref, work_ref, coef_ref, 2)
    along_y(work_ref, ends_ref, pair_ref, 10, 5)
    fill_pairs(coef_ref, pair_ref, True)

    def along_z(step, carry):
        i = step // 5 * 2
        tile = step - step // 5 * 5
        bases = [pl.multiple_of((i + g) * W_ROWS + tile * 8, 8) for g in range(2)]
        sums = [value_ref[i + g] + value_ref[30 + tile] for g in range(2)]
        data = []
        for g in range(2):
            planes = [ends_ref[pl.ds(bases[g], 8), :]]
            planes += [inner_ref[pl.ds(bases[g] + k * 400, 8), :] for k in range(8)]
            planes.append(ends_ref[pl.ds(bases[g] + 400, 8), :])
            data.append(planes)
        results = [[None] * 8 for _ in range(2)]
        for o in range(10):
            totals = [None, None]
            for r in range(10):
                scale = coef_ref[200 + r * 10 + o]
                for g in range(2):
                    term = scale * data[g][r]
                    totals[g] = term if r == 0 else totals[g] + term
            totals = [totals[g] / (sums[g] + value_ref[20 + o]) for g in range(2)]
            for k in range(8):
                scale = coef_ref[200 + (k + 1) * 10 + o]
                for g in range(2):
                    term = scale * totals[g]
                    results[g][k] = term if o == 0 else results[g][k] + term
        for g in range(2):
            for k in range(8):
                two_ref[pl.ds(bases[g] + k * 400, 8), :] = results[g][k]
        return carry

    lax.fori_loop(0, 25, along_z, 0)
    along_y(two_ref, one_ref, pair_ref, 40, 4)

    def back_x(k, carry):
        base = pl.multiple_of(k * 320, 8)
        target = pl.multiple_of(k * 256, 8)

        def load(r, t):
            return one_ref[pl.ds(base + r * INNER + t * 8, 8), :]

        def store(o, t, value):
            two_ref[pl.ds(target + o * INNER + t * 8, 8), :] = value

        contract(load, store, lambda r, o: coef_ref[(o + 1) * 10 + r], 8, 4, 4)
        return carry

    lax.fori_loop(0, 8, back_x, 0)

    for k in range(8):
        lanes = slice(k * 128, k * 128 + 128)
        for n in range(4):
            for i in range(0, 8, 2):
                pieces = [two_ref[pl.ds(k * 256 + (i + g) * INNER + n, 8, stride=4), :] for g in range(2)]
                high, low = split2(jnp.concatenate(pieces, axis=0))
                row = n * 64 + i * 8
                back_ref[row : row + 16, lanes] = high
                back_ref[256 + row : 272 + row, lanes] = low

    row = iota((1024, 128), 0)
    element = jnp.bitwise_and(row, 127)
    place = lax.shift_right_logical(element, 4) * 128 + jnp.bitwise_and(element, 15) * 8 + lax.shift_right_logical(row, 7)
    lane = iota((1024, 128), 1)
    for a in range(4):
        moves = [jnp.where(place == lane + (a * 2 + b) * 128, 1.0, 0.0).astype(BF16) for b in range(2)]
        moved = dot_n(back_ref[...], jnp.concatenate(moves, axis=1))
        moved = moved[0:256] + moved[256:512]
        for b in range(2):
            for n in range(4):
                for i in range(8):
                    first = n * 64 + i * 8
                    out_ref[n, a * 8 + i, b * 8 : b * 8 + 8, :] = moved[first : first + 8, b * 128 : b * 128 + 128]


def pairs(axis):
    size = lax.axis_size(axis)
    up = [(i, (i + 1) % size) for i in range(size)]
    return up, [(j, i) for i, j in up]


def exchange(last, leading, axis):
    up, down = pairs(axis)
    return lax.ppermute(last, axis, up), lax.ppermute(leading, axis, down)


def arrange(residual, x_before, x_after, y_before, y_after, after):
    shape = jax.ShapeDtypeStruct
    return pl.pallas_call(
        arrange_kernel,
        out_shape=(shape((3200, 128), F32), shape((32, 128), F32), shape((32, 128), F32)),
        in_specs=[pl.BlockSpec(memory_space=pltpu.SMEM)] + [pl.BlockSpec(memory_space=pltpu.VMEM)] * 5 + [pl.BlockSpec(memory_space=pl.ANY)],
        scratch_shapes=[pltpu.VMEM((4, 4, 40, 128), F32), pltpu.VMEM((896, 1024), BF16)],
        compiler_params=params(24),
        name="arrange",
    )(inner_sides("gy"), residual, x_before, x_after, y_before, y_after, after)


def forward(windows, fdm_vectors):
    return pl.pallas_call(
        forward_kernel,
        out_shape=jax.ShapeDtypeStruct((3200, 128), F32),
        scratch_shapes=[pltpu.VMEM((200, 8, 128), F32), pltpu.VMEM((50, 8, 128), F32), pltpu.VMEM((3200, 128), F32)],
        compiler_params=params(16),
        name="forward",
    )(windows, fdm_vectors)


def solve(windows, inner, z_before, z_after, fdm_vectors, fdm_values, shape):
    return pl.pallas_call(
        solve_kernel,
        out_shape=jax.ShapeDtypeStruct(shape, F32),
        in_specs=[pl.BlockSpec(memory_space=pltpu.SMEM)] + [pl.BlockSpec(memory_space=pltpu.VMEM)] * 6,
        scratch_shapes=[
            pltpu.VMEM((300, 8, 128), F32),
            pltpu.VMEM((50, 8, 128), F32),
            pltpu.VMEM((35, 8, 128), F32),
            pltpu.VMEM((800, 128), F32),
            pltpu.VMEM((800, 128), F32),
            pltpu.VMEM((2560, 128), F32),
            pltpu.VMEM((3200, 128), F32),
            pltpu.VMEM((512, 1024), BF16),
        ],
        compiler_params=params(20),
        name="solve",
    )(inner_sides("gz"), windows, inner, z_before, z_after, fdm_vectors, fdm_values)


def body(residual, fdm_vectors, fdm_values, corner_vertex, own_factor, sep_factor, sep_cols):
    x_before, x_after = exchange(residual[:, -1], residual[:, 0], "gx")
    parts, rhs = coarse_start(residual, corner_vertex, sep_factor, sep_cols)
    parts = lax.all_to_all(parts, AXES, 0, 0)
    y_last = jnp.concatenate([x_before[:, None, -1], residual[:, :, -1], x_after[:, None, -1]], axis=1)
    y_leading = jnp.concatenate([x_before[:, None, 0], residual[:, :, 0], x_after[:, None, 0]], axis=1)
    rhs, y_last, y_leading = lax.optimization_barrier((rhs, y_last, y_leading))
    y_before, y_after = exchange(y_last, y_leading, "gy")
    own_coef = jnp.einsum("vw,nv->nw", own_factor, rhs, precision=HIGH)
    own = jnp.einsum("vw,nw->nv", own_factor, own_coef, precision=HIGH)
    windows, z_last, z_leading = arrange(residual, x_before, x_after, y_before, y_after, own)
    z_before, z_after = exchange(z_last, z_leading, "gz")
    parts = middle_sums(parts, z_last)
    parts = lax.all_to_all(parts, AXES, 0, 0)
    fdm_vectors = fdm_vectors.transpose(1, 2, 0, 3)
    fdm_values = fdm_values.transpose(1, 0, 2)
    inner = forward(windows, fdm_vectors)
    local_part = solve(windows, inner, z_before, z_after, fdm_vectors, fdm_values, residual.shape)
    return coarse_end(parts, own, sep_cols, sep_factor, corner_vertex, local_part)


def solution(mesh):
    return jax.shard_map(
        body,
        mesh=mesh,
        in_specs=(
            P(None, AXES[0], AXES[1], AXES[2]),
            P(None, None, None, AXES),
            P(None, None, AXES),
            P(None, AXES),
            P(AXES, None),
            P(AXES, None),
            P(AXES, None),
        ),
        out_specs=P(None, AXES[0], AXES[1], AXES[2]),
        check_vma=False,
    )
```

```python
import functools

import jax
import jax.numpy as jnp
from jax import lax
from jax.experimental import pallas as pl
from jax.experimental.pallas import tpu as pltpu
from jax.sharding import PartitionSpec as P

NODE = 8
VERTS = 512
LINE_SEP = 1024
PLANE_SEP = 4096
AXES = ("gx", "gy", "gz")
F32 = jnp.float32
BF16 = jnp.bfloat16
HIGH = lax.Precision.HIGHEST
MIB = 1024 * 1024


def iota(shape, dim):
    return lax.broadcasted_iota(jnp.int32, shape, dim)


def split2(x):
    high = x.astype(BF16)
    return high, (x - high.astype(F32)).astype(BF16)


def dot_t(left, right):
    return lax.dot_general(left, right, (((1,), (1,)), ((), ())), preferred_element_type=F32)


def dot_n(left, right):
    return lax.dot_general(left, right, (((1,), (0,)), ((), ())), preferred_element_type=F32)


def z_weights():
    z = iota((128, 256), 0)
    col = iota((128, 256), 1)
    one = (z % NODE).astype(F32) / (NODE - 1)
    value = jnp.where(col // 128 == 1, one, 1.0 - one)
    return jnp.where(z // NODE == col % 16, value, 0.0)


def one_hot_corners(corner_ref, p, q):
    vertex = iota((VERTS, 128), 0)
    first = p * 4 + q * 2
    sides = [jnp.where(vertex == corner_ref[first + r : first + r + 1, :], 1.0, 0.0).astype(BF16) for r in range(2)]
    return jnp.concatenate(sides, axis=1)


def tile_rows(row):
    return jnp.broadcast_to(row, (16, VERTS)).astype(BF16)


def row_masks(index, rows):
    offset = tile_rows(index.astype(F32)) - iota((16, VERTS), 0).astype(F32).astype(BF16)
    return [offset == jnp.full((16, VERTS), 16.0 * r, BF16) for r in range(rows // 16)]


def one_hot(index, rows):
    one = jnp.ones((16, VERTS), BF16)
    return jnp.concatenate([pick(mask, one) for mask in row_masks(index, rows)], axis=0)


def pick(mask, value):
    return jnp.where(mask, value, jnp.zeros_like(value))


def scatter_step(col, fac, rhs, low_bits, high_rows):
    low_hot = one_hot(jnp.bitwise_and(col, (1 << low_bits) - 1), 1 << low_bits)
    masks = row_masks(lax.shift_right_logical(col, low_bits), high_rows)
    tops, rests = [], []
    for n in range(4):
        value = fac * rhs[n : n + 1, :]
        high = value.astype(BF16).astype(F32)
        high_tile, low_tile = tile_rows(high), tile_rows(value - high)
        tops += [pick(mask, high_tile) for mask in masks]
        rests += [pick(mask, low_tile) for mask in masks]
    return jnp.concatenate(tops + rests, axis=0), low_hot


def loads_kernel(
    res_hbm, corner_ref, fac_hbm, col_hbm, out_ref, rhs_ref, rows_ref, top_ref, plane_ref, line_ref, res_ref, fac_ref, col_ref, col_t_ref, fac_t_ref, sems
):
    fields = [pltpu.make_async_copy(res_hbm.at[n], res_ref.at[n], sems.at[n]) for n in range(4)]
    col_copy = pltpu.make_async_copy(col_hbm, col_ref, sems.at[4])
    fac_copy = pltpu.make_async_copy(fac_hbm, fac_ref, sems.at[5])
    for copy in fields + [col_copy, fac_copy]:
        copy.start()
    node = iota((NODE, 128), 0).astype(F32) / (NODE - 1)
    for n in range(4):
        fields[n].wait()
        for a in range(4):
            for b in range(2):
                one = zero = None
                for i in range(NODE):
                    tile = res_ref[n, a * 8 + i, b * 8 : b * 8 + 8, :]
                    if i < NODE - 1:
                        term = tile * (1.0 - i / 7.0)
                        zero = term if zero is None else zero + term
                    if i > 0:
                        term = tile * (i / 7.0)
                        one = term if one is None else one + term
                for p, part in enumerate((zero, one)):
                    row = (p * 4 + n) * 8 + a * 2 + b
                    upper = part * node
                    rows_ref[0, row : row + 1, :] = jnp.sum(part - upper, axis=0, keepdims=True)
                    rows_ref[1, row : row + 1, :] = jnp.sum(upper, axis=0, keepdims=True)
    weights = z_weights()
    own_block = iota((64, 256), 0) % 8 == (iota((64, 256), 1) % 128) // 16
    sums = [None, None]
    for q in range(2):
        spread_out = lax.dot_general(rows_ref[q], weights, (((1,), (0,)), ((), ())), precision=HIGH, preferred_element_type=F32)
        load = jnp.sum(jnp.where(own_block, spread_out, 0.0).reshape(8, 8, 256), axis=1)
        load_high, load_low = split2(load)
        left = jnp.concatenate([load_high, load_low], axis=0)
        for p in range(2):
            part = dot_t(left, one_hot_corners(corner_ref, p, q))
            sums[p] = part if sums[p] is None else sums[p] + part
    rhs = sums[0][0:4] + sums[0][8:12] + sums[1][4:8] + sums[1][12:16]
    rhs_ref[...] = rhs
    col_copy.wait()
    col_t_ref[...] = col_ref[...].T
    fac_copy.wait()
    fac_t_ref[...] = fac_ref[...].T

    top_ref[...] = jnp.zeros_like(top_ref)
    plane_ref[...] = jnp.zeros_like(plane_ref)
    line_ref[...] = jnp.zeros_like(line_ref)

    def run(first, count, unroll, base, low_bits, high_rows, total_ref):
        def body(step, carry):
            lefts, rights = [], []
            for u in range(unroll):
                m = first + step * unroll + u
                col = col_t_ref[pl.ds(m, 1), :] - base
                fac = fac_t_ref[pl.ds(m, 1), :]
                left, right = scatter_step(col, fac, rhs_ref, low_bits, high_rows)
                lefts.append(left)
                rights.append(right)
            total_ref[...] += dot_t(jnp.concatenate(lefts, axis=1), jnp.concatenate(rights, axis=1))
            return carry

        lax.fori_loop(0, count // unroll, body, 0)

    run(64, 64, 16, LINE_SEP + PLANE_SEP, 8, 64, top_ref)
    run(32, 32, 16, LINE_SEP, 8, 16, plane_ref)
    run(0, 32, 16, 0, 6, 16, line_ref)

    out_ref[...] = jnp.zeros_like(out_ref)
    flat = out_ref.reshape(1024, 128)
    for t in range(32):
        for h in range(2):
            lanes = slice(h * 128, h * 128 + 128)
            tile = top_ref[t * 8 : t * 8 + 8, lanes] + top_ref[256 + t * 8 : 264 + t * 8, lanes]
            slot = 2 * (t * 2 + h)
            out_ref[slot, 0:4, :] = tile[0:4]
            out_ref[slot + 1, 0:4, :] = tile[4:8]
    for t in range(8):
        for h in range(2):
            lanes = slice(h * 128, h * 128 + 128)
            tile = plane_ref[t * 8 : t * 8 + 8, lanes] + plane_ref[64 + t * 8 : 72 + t * 8, lanes]
            flat[pl.ds((t * 2 + h) * 64 + 4, 8, stride=8), :] = tile
    for t in range(8):
        tile = line_ref[t * 8 : t * 8 + 8, :] + line_ref[64 + t * 8 : 72 + t * 8, :]
        flat[pl.ds(t * 64 + 5, 8, stride=8), 0:64] = tile


def sums_kernel(in_ref, order_ref, out_ref):
    row = iota((8, 128), 0)
    planes, lines = [], []
    for i in range(8):
        group = []
        for j in range(4):
            first = (i * 4 + j) * 4
            group.append((in_ref[first] + in_ref[first + 1]) + (in_ref[first + 2] + in_ref[first + 3]))
        lines.append(group)
        planes.append((group[0] + group[1]) + (group[2] + group[3]))
    top = ((planes[0] + planes[1]) + (planes[2] + planes[3])) + ((planes[4] + planes[5]) + (planes[6] + planes[7]))
    for i in range(8):
        for j in range(4):
            value = jnp.where(row < 4, top, jnp.where(row == 4, planes[i], lines[i][j]))
            for k in range(4):
                out_ref[(i * 4 + j) * 4 + k] = value


def gather_step(table, col, fac, low_bits, high_rows, totals):
    found = dot_n(table, one_hot(jnp.bitwise_and(col, (1 << low_bits) - 1), 1 << low_bits))
    high = lax.shift_right_logical(col, low_bits)
    offset = jnp.broadcast_to(high, (8, VERTS)) - iota((8, VERTS), 0)
    result = []
    for n in range(4):
        total = None
        for r in range(high_rows // 8):
            first = n * high_rows + r * 8
            value = found[first : first + 8] + found[4 * high_rows + first : 4 * high_rows + first + 8]
            total = jnp.where(offset == 8 * r, value, 0.0 if total is None else total)
        result.append(totals[n] + total * fac)
    return tuple(result)


def finish_kernel(
    sep_ref, own_ref, col_ref, fac_ref, corner_ref, local_ref, out_ref, top_ref, plane_ref, line_ref, split_ref, col_t_ref, fac_t_ref
):
    col_t_ref[...] = col_ref[...].T
    fac_t_ref[...] = fac_ref[...].T
    flat = sep_ref.reshape(1024, 128)

    def put(table_ref, rows, lanes, offset, value):
        high, low = split2(value)
        table_ref[rows, lanes] = high.astype(table_ref.dtype)
        table_ref[slice(rows.start + offset, rows.stop + offset), lanes] = low.astype(table_ref.dtype)

    for t in range(32):
        for h in range(2):
            lanes = slice(h * 128, h * 128 + 128)
            slot = 2 * (t * 2 + h)
            tile = jnp.concatenate([sep_ref[slot, 0:4, :], sep_ref[slot + 1, 0:4, :]], axis=0)
            put(top_ref, slice(t * 8, t * 8 + 8), lanes, 256, tile)
    for t in range(8):
        for h in range(2):
            lanes = slice(h * 128, h * 128 + 128)
            tile = flat[pl.ds((t * 2 + h) * 64 + 4, 8, stride=8), :]
            put(plane_ref, slice(t * 8, t * 8 + 8), lanes, 64, tile)
    for t in range(8):
        tile = flat[pl.ds(t * 64 + 5, 8, stride=8), 0:64]
        put(line_ref, slice(t * 8, t * 8 + 8), slice(0, 64), 64, tile)

    def run(first, count, unroll, base, low_bits, high_rows, table_ref, totals):
        table = table_ref[...].astype(BF16)

        def body(step, carry):
            for u in range(unroll):
                m = first + step * unroll + u
                col = col_t_ref[pl.ds(m, 1), :] - base
                fac = fac_t_ref[pl.ds(m, 1), :]
                carry = gather_step(table, col, fac, low_bits, high_rows, carry)
            return carry

        return lax.fori_loop(0, count // unroll, body, totals)

    totals = tuple(jnp.zeros((8, VERTS), F32) for _ in range(4))
    totals = run(0, 32, 16, 0, 6, 16, line_ref, totals)
    totals = run(32, 32, 16, LINE_SEP, 8, 16, plane_ref, totals)
    totals = run(64, 64, 16, LINE_SEP + PLANE_SEP, 8, 64, top_ref, totals)
    for n in range(4):
        value = jnp.sum(totals[n], axis=0, keepdims=True) + own_ref[n : n + 1, :]
        high, low = split2(value)
        split_ref[n : n + 1, :] = high.astype(F32)
        split_ref[n + 4 : n + 5, :] = low.astype(F32)
    left = split_ref[...].astype(BF16)
    left = jnp.concatenate([left, jnp.zeros_like(left)], axis=0)
    weights = z_weights()
    node = iota((NODE, 128), 0).astype(F32) / (NODE - 1)
    own_block = iota((8, 256), 0) == (iota((8, 256), 1) % 128) // 16
    edges = []
    for p in range(2):
        for q in range(2):
            corners = dot_n(left, one_hot_corners(corner_ref, p, q))
            rows = []
            for n in range(4):
                value = corners[n : n + 1, :] + corners[n + 4 : n + 5, :]
                rows.append(jnp.where(own_block, jnp.broadcast_to(value, (8, 256)), 0.0))
            edges.append(
                lax.dot_general(jnp.concatenate(rows, axis=0), weights, (((1,), (1,)), ((), ())), precision=HIGH, preferred_element_type=F32)
            )
    for n in range(4):
        for a in range(4):
            for b in range(2):
                row = n * 8 + a * 2 + b
                ends = []
                for p in range(2):
                    at_zero = edges[p * 2][row : row + 1, :]
                    step = edges[p * 2 + 1][row : row + 1, :] - at_zero
                    ends.append(at_zero + node * step)
                step = ends[1] - ends[0]
                for i in range(NODE):
                    tile = local_ref[n, a * 8 + i, b * 8 : b * 8 + 8, :]
                    out_ref[n, a * 8 + i, b * 8 : b * 8 + 8, :] = tile + (ends[0] + step * (i / 7.0))


def params(mib):
    return pltpu.CompilerParams(vmem_limit_bytes=mib * MIB)


def coarse_start(residual, corner_vertex, sep_factor, sep_cols):
    shape = jax.ShapeDtypeStruct
    return pl.pallas_call(
        loads_kernel,
        out_shape=(shape((128, 8, 128), F32), shape((4, VERTS), F32)),
        in_specs=[
            pl.BlockSpec(memory_space=pl.ANY),
            pl.BlockSpec(memory_space=pltpu.VMEM),
            pl.BlockSpec(memory_space=pl.ANY),
            pl.BlockSpec(memory_space=pl.ANY),
        ],
        scratch_shapes=[
            pltpu.VMEM((2, 64, 128), F32),
            pltpu.VMEM((512, 256), F32),
            pltpu.VMEM((128, 256), F32),
            pltpu.VMEM((128, 64), F32),
            pltpu.VMEM((4, 32, 16, 128), F32),
            pltpu.VMEM((512, 128), F32),
            pltpu.VMEM((512, 128), jnp.int32),
            pltpu.VMEM((128, VERTS), jnp.int32),
            pltpu.VMEM((128, VERTS), F32),
            pltpu.SemaphoreType.DMA((6,)),
        ],
        compiler_params=params(60),
        name="loads",
    )(residual, corner_vertex, sep_factor, sep_cols)


def middle_sums(parts, after):
    return pl.pallas_call(
        sums_kernel,
        out_shape=jax.ShapeDtypeStruct((128, 8, 128), F32),
        in_specs=[pl.BlockSpec(memory_space=pltpu.VMEM), pl.BlockSpec(memory_space=pl.ANY)],
        compiler_params=params(16),
        name="sums",
    )(parts, after)


def coarse_end(parts, own, sep_cols, sep_factor, corner_vertex, local_part):
    return pl.pallas_call(
        finish_kernel,
        out_shape=jax.ShapeDtypeStruct(local_part.shape, F32),
        scratch_shapes=[
            pltpu.VMEM((512, 256), F32),
            pltpu.VMEM((128, 256), F32),
            pltpu.VMEM((128, 64), F32),
            pltpu.VMEM((8, VERTS), F32),
            pltpu.VMEM((128, VERTS), jnp.int32),
            pltpu.VMEM((128, VERTS), F32),
        ],
        compiler_params=params(32),
        name="finish",
    )(parts, own, sep_cols, sep_factor, corner_vertex, local_part)


W_ROWS = 40
INNER = 32


def inner_sides(axis):
    index = lax.axis_index(axis)
    return jnp.stack([index > 0, index < lax.axis_size(axis) - 1]).astype(F32)


def masked(flag, value):
    return jnp.where(flag > 0.5, value, 0.0)


def put_left(left_ref, half, row, block, value):
    high, low = split2(value)
    lanes = slice(block * 128, block * 128 + 128)
    left_ref[row : row + 16, lanes] = high
    left_ref[half + row : half + row + 16, lanes] = low


def moved_pairs(left_ref, half):
    row = iota((1024, 128), 0)
    z = jnp.bitwise_and(row, 127)
    place = jnp.bitwise_and(z, 7) * 128 + lax.shift_right_logical(row, 7) * 16 + lax.shift_right_logical(z, 3)
    lane = iota((1024, 128), 1)
    for pair in range(4):
        moves = [jnp.where(place == lane + (pair * 2 + h) * 128, 1.0, 0.0).astype(BF16) for h in range(2)]
        moved = dot_n(left_ref[...], jnp.concatenate(moves, axis=1))
        yield pair, moved[0:half] + moved[half : 2 * half]


def core_kernel(res_ref, x_before_ref, x_after_ref, core_ref, edge_ref, left_ref):
    flat = res_ref.reshape(2048, 128)
    for n in range(4):
        for side, y in ((0, 7), (1, 8)):
            edge_ref[side, n, 0:1, :] = x_before_ref[n, y : y + 1, :]
            edge_ref[side, n, 1:33, :] = flat[pl.ds(n * 512 + y, 32, stride=16), :]
            edge_ref[side, n, 33:34, :] = x_after_ref[n, y : y + 1, :]
            edge_ref[side, n, 34:40, :] = jnp.zeros((6, 128), F32)

    def tile(n, x, b):
        rows = slice(b * 8, b * 8 + 8)
        if x < 0:
            return x_before_ref[n, rows, :]
        if x > 31:
            return x_after_ref[n, rows, :]
        return res_ref[n, x, rows, :]

    for n in range(4):
        for a in range(4):
            for b in range(2):
                for i in range(0, 10, 2):
                    x = a * 8 + i - 1
                    put_left(left_ref, 320, n * 80 + i * 8, a * 2 + b, jnp.concatenate([tile(n, x, b), tile(n, x + 1, b)], axis=0))
    for pair, moved in moved_pairs(left_ref, 320):
        for h in range(2):
            base = (pair * 2 + h) * 400
            lanes = slice(h * 128, h * 128 + 128)
            for n in range(4):
                for i in range(10):
                    first = n * 80 + i * 8
                    core_ref[pl.ds(base + i * W_ROWS + 4 + n, 8, stride=4), :] = moved[first : first + 8, lanes]


def arrange_kernel(flag_ref, core_ref, own_edge_ref, y_before_ref, y_after_ref, order_ref, win_ref, high_ref, low_ref, edge_ref, left_ref):
    for n in range(4):
        edge_ref[0, n, 0:34, :] = masked(flag_ref[0], y_before_ref[n])
        edge_ref[0, n, 34:40, :] = jnp.zeros((6, 128), F32)
        edge_ref[1, n] = own_edge_ref[0, n]
        edge_ref[2, n] = own_edge_ref[1, n]
        edge_ref[3, n, 0:34, :] = masked(flag_ref[1], y_after_ref[n])
        edge_ref[3, n, 34:40, :] = jnp.zeros((6, 128), F32)
    for n in range(4):
        for a in range(4):
            for b in range(2):
                for side in range(2):
                    put_left(left_ref, 128, (n * 2 + side) * 16, a * 2 + b, edge_ref[side * 2 + b, n, a * 8 : a * 8 + 16, :])
    win_ref[...] = core_ref[...]
    for pair, moved in moved_pairs(left_ref, 128):
        for h in range(2):
            base = (pair * 2 + h) * 400
            lanes = slice(h * 128, h * 128 + 128)
            for n in range(4):
                for side in range(2):
                    first = (n * 2 + side) * 16
                    start = base + side * 36 + n
                    win_ref[pl.ds(start, 8, stride=W_ROWS), :] = moved[first : first + 8, lanes]
                    win_ref[start + 320 : start + 321, :] = moved[first + 8 : first + 9, lanes]
                    win_ref[start + 360 : start + 361, :] = moved[first + 9 : first + 10, lanes]

    spot = jnp.bitwise_and(iota((8, 128), 1), 15)
    for group in range(4):
        high = jnp.zeros((8, 128), F32)
        low = jnp.zeros((8, 128), F32)
        for t in range(16):
            at = group * 16 + t
            if at < 50:
                top = win_ref[2800 + at * 8 : 2808 + at * 8, :]
                high = jnp.where(spot == t, pltpu.roll(top, (t - 15) % 128, 1), high)
                bottom = win_ref[at * 8 : at * 8 + 8, :]
                low = jnp.where(spot == t, pltpu.roll(bottom, t, 1), low)
        high_ref[group * 8 : group * 8 + 8, :] = high
        low_ref[group * 8 : group * 8 + 8, :] = low


EIGHT = (8, 128)


def fill_coefficients(vec_ref, coef_ref, dims):
    for d in dims:
        for r in range(10):
            for c in range(10):
                coef_ref[d * 100 + r * 10 + c] = jnp.broadcast_to(vec_ref[r, c, d : d + 1, :], EIGHT)


def contract(load, store, coef, outs, tiles, chunk):
    for begin in range(0, outs, chunk):
        totals = [[None] * tiles for _ in range(chunk)]
        for r in range(10):
            data = [load(r, t) for t in range(tiles)]
            for o in range(chunk):
                scale = coef(r, begin + o)
                for t in range(tiles):
                    term = scale * data[t]
                    totals[o][t] = term if r == 0 else totals[o][t] + term
        for o in range(chunk):
            for t in range(tiles):
                store(begin + o, t, totals[o][t])


def fill_pairs(coef_ref, pair_ref, back):
    first_half = iota(EIGHT, 0) < 4

    def halves(one, two):
        return jnp.where(first_half, coef_ref[100 + one[0] * 10 + one[1]], coef_ref[100 + two[0] * 10 + two[1]])

    for m in range(4 if back else 5):
        for k in range(5):
            if back:
                pair_ref[m * 10 + k * 2] = halves((2 * m + 1, 2 * k), (2 * m + 2, 2 * k + 1))
                pair_ref[m * 10 + k * 2 + 1] = halves((2 * m + 1, 2 * k + 1), (2 * m + 2, 2 * k))
            else:
                pair_ref[m * 10 + k * 2] = halves((2 * k, 2 * m), (2 * k + 1, 2 * m + 1))
                pair_ref[m * 10 + k * 2 + 1] = halves((2 * k + 1, 2 * m), (2 * k, 2 * m + 1))


def along_y(source_ref, target_ref, pair_ref, steps, tiles):
    def body(step, carry):
        data = []
        for g in range(2):
            base = pl.multiple_of((step * 2 + g) * W_ROWS, 8)
            plain = [source_ref[pl.ds(base + t * 8, 8), :] for t in range(5)]
            data.append([(v, pltpu.roll(v, 4, 0)) for v in plain])
        for m in range(tiles):
            totals = [None, None]
            for r in range(5):
                for c in range(2):
                    scale = pair_ref[m * 10 + r * 2 + c]
                    for g in range(2):
                        term = scale * data[g][r][c]
                        totals[g] = term if totals[g] is None else totals[g] + term
            for g in range(2):
                target = pl.multiple_of((step * 2 + g) * tiles * 8, 8)
                target_ref[pl.ds(target + m * 8, 8), :] = totals[g]
        return carry

    lax.fori_loop(0, steps, body, 0)


def along_x(source_ref, target_ref, coef_ref, planes):
    def body(k, carry):
        base = pl.multiple_of(k * 400, 8)

        def load(r, t):
            return source_ref[pl.ds(base + r * W_ROWS + t * 8, 8), :]

        def store(o, t, value):
            target_ref[pl.ds(base + o * W_ROWS + t * 8, 8), :] = value

        contract(load, store, lambda r, o: coef_ref[r * 10 + o], 10, 5, 5)
        return carry

    lax.fori_loop(0, planes, body, 0)


def forward_kernel(win_ref, vec_ref, out_ref, coef_ref, pair_ref, work_ref):
    fill_coefficients(vec_ref, coef_ref, (0, 1))
    fill_pairs(coef_ref, pair_ref, False)
    along_x(win_ref, work_ref, coef_ref, 8)
    along_y(work_ref, out_ref, pair_ref, 40, 5)


def solve_kernel(flag_ref, win_ref, inner_ref, before_ref, after_ref, vec_ref, val_ref, out_ref, coef_ref, pair_ref, value_ref, ends_ref, work_ref, one_ref, two_ref, back_ref):
    fill_coefficients(vec_ref, coef_ref, (0, 1, 2))
    fill_pairs(coef_ref, pair_ref, False)
    first_half = iota(EIGHT, 0) < 4
    for d in range(3):
        for r in range(10):
            value_ref[d * 10 + r] = jnp.broadcast_to(val_ref[r, d : d + 1, :], EIGHT)
    for m in range(5):
        value_ref[30 + m] = jnp.where(first_half, value_ref[10 + 2 * m], value_ref[11 + 2 * m])

    spot = jnp.bitwise_and(iota(EIGHT, 1), 15)
    for at in range(50):
        group = slice(at // 16 * 8, at // 16 * 8 + 8)
        t = at % 16
        rows = slice(at * 8, at * 8 + 8)
        inside = pltpu.roll(win_ref[2800 + at * 8 : 2808 + at * 8, :], 1, 1)
        outside = masked(flag_ref[0], pltpu.roll(before_ref[group, :], (-t) % 128, 1))
        ends_ref[rows, :] = jnp.where(spot == 0, outside, inside)
        inside = pltpu.roll(win_ref[rows, :], 127, 1)
        outside = masked(flag_ref[1], pltpu.roll(after_ref[group, :], 15 - t, 1))
        ends_ref[400 + at * 8 : 408 + at * 8, :] = jnp.where(spot == 15, outside, inside)
    along_x(ends_ref, work_ref, coef_ref, 2)
    along_y(work_ref, ends_ref, pair_ref, 10, 5)
    fill_pairs(coef_ref, pair_ref, True)

    def along_z(step, carry):
        i = step // 5 * 2
        tile = step - step // 5 * 5
        bases = [pl.multiple_of((i + g) * W_ROWS + tile * 8, 8) for g in range(2)]
        sums = [value_ref[i + g] + value_ref[30 + tile] for g in range(2)]
        data = []
        for g in range(2):
            planes = [ends_ref[pl.ds(bases[g], 8), :]]
            planes += [inner_ref[pl.ds(bases[g] + k * 400, 8), :] for k in range(8)]
            planes.append(ends_ref[pl.ds(bases[g] + 400, 8), :])
            data.append(planes)
        results = [[None] * 8 for _ in range(2)]
        for o in range(10):
            totals = [None, None]
            for r in range(10):
                scale = coef_ref[200 + r * 10 + o]
                for g in range(2):
                    term = scale * data[g][r]
                    totals[g] = term if r == 0 else totals[g] + term
            totals = [totals[g] / (sums[g] + value_ref[20 + o]) for g in range(2)]
            for k in range(8):
                scale = coef_ref[200 + (k + 1) * 10 + o]
                for g in range(2):
                    term = scale * totals[g]
                    results[g][k] = term if o == 0 else results[g][k] + term
        for g in range(2):
            for k in range(8):
                two_ref[pl.ds(bases[g] + k * 400, 8), :] = results[g][k]
        return carry

    lax.fori_loop(0, 25, along_z, 0)
    along_y(two_ref, one_ref, pair_ref, 40, 4)

    def back_x(k, carry):
        base = pl.multiple_of(k * 320, 8)
        target = pl.multiple_of(k * 256, 8)

        def load(r, t):
            return one_ref[pl.ds(base + r * INNER + t * 8, 8), :]

        def store(o, t, value):
            two_ref[pl.ds(target + o * INNER + t * 8, 8), :] = value

        contract(load, store, lambda r, o: coef_ref[(o + 1) * 10 + r], 8, 4, 4)
        return carry

    lax.fori_loop(0, 8, back_x, 0)

    for k in range(8):
        lanes = slice(k * 128, k * 128 + 128)
        for n in range(4):
            for i in range(0, 8, 2):
                pieces = [two_ref[pl.ds(k * 256 + (i + g) * INNER + n, 8, stride=4), :] for g in range(2)]
                high, low = split2(jnp.concatenate(pieces, axis=0))
                row = n * 64 + i * 8
                back_ref[row : row + 16, lanes] = high
                back_ref[256 + row : 272 + row, lanes] = low

    row = iota((1024, 128), 0)
    element = jnp.bitwise_and(row, 127)
    place = lax.shift_right_logical(element, 4) * 128 + jnp.bitwise_and(element, 15) * 8 + lax.shift_right_logical(row, 7)
    lane = iota((1024, 128), 1)
    for a in range(4):
        moves = [jnp.where(place == lane + (a * 2 + b) * 128, 1.0, 0.0).astype(BF16) for b in range(2)]
        moved = dot_n(back_ref[...], jnp.concatenate(moves, axis=1))
        moved = moved[0:256] + moved[256:512]
        for b in range(2):
            for n in range(4):
                for i in range(8):
                    first = n * 64 + i * 8
                    out_ref[n, a * 8 + i, b * 8 : b * 8 + 8, :] = moved[first : first + 8, b * 128 : b * 128 + 128]


def pairs(axis):
    size = lax.axis_size(axis)
    up = [(i, (i + 1) % size) for i in range(size)]
    return up, [(j, i) for i, j in up]


def exchange(last, leading, axis):
    up, down = pairs(axis)
    return lax.ppermute(last, axis, up), lax.ppermute(leading, axis, down)


def core(residual, x_before, x_after):
    shape = jax.ShapeDtypeStruct
    return pl.pallas_call(
        core_kernel,
        out_shape=(shape((3200, 128), F32), shape((2, 4, 40, 128), F32)),
        scratch_shapes=[pltpu.VMEM((640, 1024), BF16)],
        compiler_params=params(24),
        name="core",
    )(residual, x_before, x_after)


def arrange(inside, own_edges, y_before, y_after, after):
    shape = jax.ShapeDtypeStruct
    return pl.pallas_call(
        arrange_kernel,
        out_shape=(shape((3200, 128), F32), shape((32, 128), F32), shape((32, 128), F32)),
        in_specs=[pl.BlockSpec(memory_space=pltpu.SMEM)] + [pl.BlockSpec(memory_space=pltpu.VMEM)] * 4 + [pl.BlockSpec(memory_space=pl.ANY)],
        scratch_shapes=[pltpu.VMEM((4, 4, 40, 128), F32), pltpu.VMEM((256, 1024), BF16)],
        compiler_params=params(24),
        name="arrange",
    )(inner_sides("gy"), inside, own_edges, y_before, y_after, after)


def forward(windows, fdm_vectors):
    return pl.pallas_call(
        forward_kernel,
        out_shape=jax.ShapeDtypeStruct((3200, 128), F32),
        scratch_shapes=[pltpu.VMEM((200, 8, 128), F32), pltpu.VMEM((50, 8, 128), F32), pltpu.VMEM((3200, 128), F32)],
        compiler_params=params(16),
        name="forward",
    )(windows, fdm_vectors)


def solve(windows, inner, z_before, z_after, fdm_vectors, fdm_values, shape):
    return pl.pallas_call(
        solve_kernel,
        out_shape=jax.ShapeDtypeStruct(shape, F32),
        in_specs=[pl.BlockSpec(memory_space=pltpu.SMEM)] + [pl.BlockSpec(memory_space=pltpu.VMEM)] * 6,
        scratch_shapes=[
            pltpu.VMEM((300, 8, 128), F32),
            pltpu.VMEM((50, 8, 128), F32),
            pltpu.VMEM((35, 8, 128), F32),
            pltpu.VMEM((800, 128), F32),
            pltpu.VMEM((800, 128), F32),
            pltpu.VMEM((2560, 128), F32),
            pltpu.VMEM((3200, 128), F32),
            pltpu.VMEM((512, 1024), BF16),
        ],
        compiler_params=params(20),
        name="solve",
    )(inner_sides("gz"), windows, inner, z_before, z_after, fdm_vectors, fdm_values)


def body(residual, fdm_vectors, fdm_values, corner_vertex, own_factor, sep_factor, sep_cols):
    x_before, x_after = exchange(residual[:, -1], residual[:, 0], "gx")
    parts, rhs = coarse_start(residual, corner_vertex, sep_factor, sep_cols)
    parts = lax.all_to_all(parts, AXES, 0, 0)
    y_last = jnp.concatenate([x_before[:, None, -1], residual[:, :, -1], x_after[:, None, -1]], axis=1)
    y_leading = jnp.concatenate([x_before[:, None, 0], residual[:, :, 0], x_after[:, None, 0]], axis=1)
    rhs, y_last, y_leading, x_before, x_after = lax.optimization_barrier((rhs, y_last, y_leading, x_before, x_after))
    y_before, y_after = exchange(y_last, y_leading, "gy")
    own_coef = jnp.einsum("vw,nv->nw", own_factor, rhs, precision=HIGH)
    own = jnp.einsum("vw,nw->nv", own_factor, own_coef, precision=HIGH)
    inside, own_edges = core(residual, x_before, x_after)
    windows, z_last, z_leading = arrange(inside, own_edges, y_before, y_after, own)
    z_before, z_after = exchange(z_last, z_leading, "gz")
    parts = middle_sums(parts, z_last)
    parts = lax.all_to_all(parts, AXES, 0, 0)
    fdm_vectors = fdm_vectors.transpose(1, 2, 0, 3)
    fdm_values = fdm_values.transpose(1, 0, 2)
    inner = forward(windows, fdm_vectors)
    local_part = solve(windows, inner, z_before, z_after, fdm_vectors, fdm_values, residual.shape)
    return coarse_end(parts, own, sep_cols, sep_factor, corner_vertex, local_part)


def solution(mesh):
    return jax.shard_map(
        body,
        mesh=mesh,
        in_specs=(
            P(None, AXES[0], AXES[1], AXES[2]),
            P(None, None, None, AXES),
            P(None, None, AXES),
            P(None, AXES),
            P(AXES, None),
            P(AXES, None),
            P(AXES, None),
        ),
        out_specs=P(None, AXES[0], AXES[1], AXES[2]),
        check_vma=False,
    )
```
